32 devices in a mesh: row: 4 (over y, x), head: 8 (over z, core).
Axes of the slice: x: 2, y: 2, z: 4, core: 2. Of those that a mesh axis runs over, the one named last changes fastest.
Arguments:
- tokens: bfloat16 [8192, 2048], P(('row', 'head')), may hold values from -6 to 6
- in_weight: bfloat16 [2048, 8512], P(('row', 'head')), may hold values from -0.125 to 0.125
- norm_gain: bfloat16 [2048], P(('row', 'head')), may hold values from 0.5 to 1.5
- out_weight: bfloat16 [4096, 2048], P(('row', 'head')), may hold values from -0.09375 to 0.09375
- gate_gain: bfloat16 [4096], P(('row', 'head')), may hold values from 0.5 to 1.5
- conv_weight: float32 [4, 4352], replicated, may hold values from -3 to 3
- conv_bias: float32 [4352], replicated, may hold values from -3 to 3
- dt_bias: float32 [64], replicated, may hold values from -7 to -1
- a_log: float32 [64], replicated, may hold values from -1 to 2.5
- skip_gain: float32 [64], replicated, may hold values from 0.5 to 1.5
- boundary: int32 [4, 2048], P('row'), may hold values 0 or 1
- fill: int32 [4], P('row'), may hold values from 1024 to 2048
- cotangent: bfloat16 [8192, 2048], P(('row', 'head')), may hold values from -6 to 6
Outputs:
- output: bfloat16 [8192, 2048], P(('row', 'head'))
- input_grad: bfloat16 [8192, 2048], P(('row', 'head'))
- in_weight_grad: float32 [2048, 8512], P(('row', 'head'))
- norm_gain_grad: float32 [2048], P(('row', 'head'))
- out_weight_grad: float32 [4096, 2048], P(('row', 'head'))
- gate_gain_grad: float32 [4096], P(('row', 'head'))
- conv_weight_grad: float32 [4, 4352], replicated
- conv_bias_grad: float32 [4352], replicated
- dt_bias_grad: float32 [64], replicated
- a_log_grad: float32 [64], replicated
- skip_gain_grad: float32 [64], replicated
The draws below stay inside these ranges and needn't reach their ends.
All inputs are finite; a program needn't handle non-finite values. No bound on the sum of `boundary` on one device may be relied on, other than what follows from the above.
Results may differ from the reference program's by a relative error of at most 0.011.
Values may be sent and summed in bfloat16 or wider, within the bound.
No kernel may reach another device: no remote copies, remote signals or barrier semaphores. Data moves between devices by JAX's collectives and lax.ppermute only.
A program may use at most 384 MiB of HBM per device.

```python
import math
from functools import partial
import jax
import jax.numpy as jnp
from jax import lax

D = 2048
HEADS = 64
NSTATE = 128
CONV = 4
SPAN = 256
SEQ = 2048
DIN = 4096
PROJ = 8512
ROWS = 4
TOKENS = 8192


def plant(values, rng, low, high):
    longest = values.shape.index(max(values.shape))
    spots = []
    for shift in (0, 1):
        where = [jax.random.randint(jax.random.fold_in(rng, axis), (), 0, length) for axis, length in enumerate(values.shape)]
        where[longest] = (where[longest] + shift) % values.shape[longest]
        spots.append(tuple(where))
    return values.at[spots[0]].set(low).at[spots[1]].set(high)


def steps_of(key, shape, cuts, low, top_value):
    gain = 1.0
    for dim, shards_of in cuts:
        heights = jax.random.uniform(jax.random.fold_in(jax.random.fold_in(key, 6), dim), (shards_of,), jnp.float32, low / len(cuts), top_value / len(cuts))
        gain = gain * jnp.repeat(jnp.exp(heights), shape[dim] // shards_of).reshape((-1,) + (1,) * (len(shape) - 1 - dim))
    return gain


def normal_values(stream_key, extent, scale, bound, split=(), kind=jnp.bfloat16):
    loudness = steps_of(stream_key, extent, split, -0.22, 0.18) if split else 1.0
    values = jax.random.normal(stream_key, extent, jnp.float32) * scale * loudness
    return jnp.minimum(jnp.maximum(values, -bound), bound).astype(kind)


def setup_inputs(seed: int = 0) -> dict:
    seeds = jax.random.split(jax.random.key(seed), 14)
    return {
        "tokens": normal_values(seeds[0], (TOKENS, D), 1.0, 6.0, ((0, 32),)),
        "in_weight": normal_values(seeds[1], (D, PROJ), D ** -0.5, 0.125, ((0, 32),)),
        "norm_gain": jnp.clip(1.0 + 0.1 * jax.random.normal(seeds[2], (D,), jnp.float32), 0.5, 1.5).astype(jnp.bfloat16),
        "out_weight": normal_values(seeds[3], (DIN, D), DIN ** -0.5, 0.09375, ((0, 32),)),
        "gate_gain": jnp.clip(1.0 + 0.1 * jax.random.normal(seeds[4], (DIN,), jnp.float32), 0.5, 1.5).astype(jnp.bfloat16),
        "conv_weight": normal_values(seeds[5], (CONV, DIN + 2 * NSTATE), CONV ** -0.5, 3.0, (), jnp.float32),
        "conv_bias": normal_values(seeds[6], (DIN + 2 * NSTATE,), 0.5, 3.0, (), jnp.float32),
        "dt_bias": jnp.clip(jax.random.uniform(seeds[7], (HEADS,), jnp.float32, -7.0, -1.0), -7.0, -1.0),
        "a_log": jnp.clip(jax.random.uniform(seeds[8], (HEADS,), jnp.float32, -1.0, 2.5), -1.0, 2.5),
        "skip_gain": jnp.clip(jax.random.uniform(seeds[9], (HEADS,), jnp.float32, 0.5, 1.5), 0.5, 1.5),
        "boundary": plant((jax.random.randint(seeds[10], (ROWS, SEQ), 0, SEQ // 4) < 1).astype(jnp.int32), jax.random.fold_in(seeds[10], 1), 0, 1),
        "fill": plant(jax.random.randint(seeds[11], (ROWS,), SEQ // 2, SEQ + 1), jax.random.fold_in(seeds[11], 1), SEQ // 2, SEQ).astype(jnp.int32),
        "cotangent": normal_values(seeds[12], (TOKENS, D), 1.0, 6.0, ((0, 32),)),
    }


epsilon = 1e-05
highest = lax.Precision.HIGHEST

@jax.custom_vjp
def low(v):
    return lax.optimization_barrier(v.astype(jnp.bfloat16)).astype(jnp.float32)

@jax.custom_vjp
def low_back(v):
    return v

def low_keep(v):
    return (low(v), None)

def low_pass(kept, grad):
    return (grad,)

def back_keep(v):
    return (v, None)

def back_low(kept, grad):
    return (low(grad),)
low.defvjp(low_keep, low_pass)
low_back.defvjp(back_keep, back_low)

def row_norm(values):
    return values * lax.rsqrt(lax.optimization_barrier(jnp.mean(values * values, axis=-1, keepdims=True)) + epsilon)

def gate_piece(mixed_heads, gate_values):
    return row_norm(mixed_heads * jax.nn.silu(gate_values))

def conv_piece(raw_values, tap_weight, tap_bias, segments):
    tap_count = tap_weight.shape[0]
    result = tap_bias + tap_weight[0] * raw_values
    for offset in range(1, tap_count):
        shifted = jnp.pad(raw_values, ((0, 0), (offset, 0), (0, 0)))[:, :-offset]
        shifted_seg = jnp.pad(segments, ((0, 0), (offset, 0)), constant_values=-1)[:, :-offset]
        usable = (shifted_seg == segments).astype(raw_values.dtype)
        result = result + tap_weight[offset] * shifted * usable[:, :, None]
    return jax.nn.silu(result)

def block_step(decay_rate, memory, inputs):
    values, step_sizes, keys_in, queries, segments, previous = inputs
    length = step_sizes.shape[1]
    log_decay = jnp.cumsum(step_sizes * decay_rate, axis=1)
    causal = jnp.arange(length)[:, None] >= jnp.arange(length)[None, :]
    linked = jnp.logical_and(segments[:, :, None] == segments[:, None, :], causal[None])[..., None]
    spread = log_decay[:, :, None, :] - log_decay[:, None, :, :]
    decays = jnp.where(linked, jnp.exp(jnp.where(linked, spread, 0.0)), 0.0)
    scores = jnp.einsum('rtn,run->rtu', queries, keys_in, precision=highest)
    scaled_values = values * step_sizes[..., None]
    within = jnp.einsum('rtuh,ruhp->rthp', decays * scores[..., None], scaled_values, precision=highest)
    carried = (segments == previous[:, None]).astype(log_decay.dtype)
    reading = jnp.einsum('rtn,rhpn->rthp', queries, memory, precision=highest)
    across = reading * (jnp.exp(log_decay) * carried[..., None])[..., None]
    ending = (segments == segments[:, -1:]).astype(log_decay.dtype)
    to_end = jnp.exp(log_decay[:, -1:, :] - log_decay) * ending[..., None]
    local_state = jnp.einsum('ruh,ruhp,run->rhpn', to_end, scaled_values, keys_in, precision=highest)
    survive = jnp.exp(log_decay[:, -1, :]) * (segments[:, -1] == previous).astype(log_decay.dtype)[:, None]
    return (survive[:, :, None, None] * memory + local_state, within + across)

def ssd_scan(values, step_sizes, decay_rate, keys_in, queries, segments, span_len):
    row_count, seq_len, head_count, head_dim = values.shape
    block_count = seq_len // span_len

    def blocks(tensor):
        return jnp.moveaxis(tensor.reshape((row_count, block_count, span_len) + tensor.shape[2:]), 1, 0)
    last_ids = segments.reshape(row_count, block_count, span_len)[:, :, -1].astype(jnp.int32)
    previous = jnp.concatenate([jnp.full((row_count, 1), -1, jnp.int32), last_ids[:, :-1]], axis=1)
    stepper = jax.checkpoint(partial(block_step, decay_rate))
    memory = jnp.zeros((row_count, head_count, head_dim, keys_in.shape[-1]), values.dtype)
    last_memory, outputs = lax.scan(stepper, memory, (blocks(values), blocks(step_sizes), blocks(keys_in), blocks(queries), blocks(segments), jnp.moveaxis(previous, 1, 0)))
    return jnp.moveaxis(outputs, 0, 1).reshape(row_count, seq_len, head_count, head_dim)

def ssd_piece(conv_values, raw_steps, step_bias, decay_log, skip_heads, segments, fill_mask, width, state_size, span_len):
    row_count, seq_len, head_count = raw_steps.shape
    head_dim = width // head_count
    values = conv_values[..., :width].reshape(row_count, seq_len, head_count, head_dim)
    keys_in = conv_values[..., width:width + state_size]
    queries = conv_values[..., width + state_size:]
    step_sizes = jax.nn.softplus(raw_steps + step_bias)
    decay_rate = -jnp.exp(decay_log)
    core = ssd_scan(values, step_sizes, decay_rate, keys_in, queries, segments, span_len)
    mixed = (core + skip_heads[:, None] * values) * fill_mask[:, :, None, None]
    return mixed.reshape(row_count, seq_len, width)

def layer(layer_input, weight_tuple, segments, fill_mask):
    in_weight, norm_gain, out_weight, gate_gain, conv_weight, conv_bias, dt_bias, a_log, skip_gain = weight_tuple
    row_count, seq_len = segments.shape
    normed = row_norm(layer_input)
    projected_in = low(normed * norm_gain)
    projected = low_back(jnp.dot(projected_in, in_weight, precision=highest, preferred_element_type=jnp.float32))
    gate_values = projected[:, :DIN]
    sent = low(projected[:, DIN:])
    conv_raw = sent[:, :DIN + 2 * NSTATE].reshape(row_count, seq_len, DIN + 2 * NSTATE)
    raw_steps = sent[:, DIN + 2 * NSTATE:].reshape(row_count, seq_len, HEADS)
    conv_values = low(conv_piece(conv_raw, conv_weight, conv_bias, segments))
    mixed = ssd_piece(conv_values, raw_steps, dt_bias, a_log, skip_gain, segments, fill_mask, DIN, NSTATE, SPAN)
    mixed = low(low_back(mixed.reshape(row_count * seq_len, DIN)))
    gated = gate_piece(mixed, gate_values)
    projected_out = low(gated * gate_gain)
    return layer_input + jnp.dot(projected_out, out_weight, precision=highest, preferred_element_type=jnp.float32)

def reference(tokens, in_weight, norm_gain, out_weight, gate_gain, conv_weight, conv_bias, dt_bias, a_log, skip_gain, boundary, fill, cotangent):
    block_rows = math.gcd(ROWS, max(1, 4096 // SEQ))
    block_count = ROWS // block_rows
    block_len = block_rows * SEQ
    segments = jnp.cumsum(boundary, axis=1).astype(jnp.int32)
    fill_mask = (jnp.arange(SEQ)[None, :] < fill[:, None]).astype(jnp.float32)
    weights = tuple((param.astype(jnp.float32) for param in (in_weight, norm_gain, out_weight, gate_gain, conv_weight, conv_bias, dt_bias, a_log, skip_gain)))

    def one_block(totals, pieces):
        block_input, block_cot, block_seg, block_fill = pieces

        def closed(layer_input, weight_tuple):
            return layer(layer_input, weight_tuple, block_seg, block_fill)
        result, back_fn = jax.vjp(closed, block_input.astype(jnp.float32), weights)
        grad_input, grad_weights = back_fn(block_cot.astype(jnp.float32))
        totals = jax.tree.map(lambda running, update: running + update, totals, grad_weights)
        return (totals, (result.astype(jnp.bfloat16), grad_input.astype(jnp.bfloat16)))
    start_totals = jax.tree.map(jnp.zeros_like, weights)
    totals, (outputs, input_grads) = lax.scan(one_block, start_totals, (tokens.reshape(block_count, block_len, D), cotangent.reshape(block_count, block_len, D), segments.reshape(block_count, block_rows, SEQ), fill_mask.reshape(block_count, block_rows, SEQ)))
    return (outputs.reshape(TOKENS, D), input_grads.reshape(TOKENS, D), totals[0], totals[1], totals[2], totals[3], totals[4], totals[5], totals[6], totals[7], totals[8])
```

```python
import jax
import jax.numpy as jnp
from jax import lax
from jax.experimental import pallas as pl
from jax.experimental.pallas import tpu as pltpu
from jax.sharding import PartitionSpec as P

HEADS = 64
HDIM = 64
NSTATE = 128
SPAN = 256
DIN = 4096
TAPS = 4
LANES = 128
epsilon = 1e-05

f32 = jnp.float32
bf16 = jnp.bfloat16

NN = (((1,), (0,)), ((), ()))
NT = (((1,), (1,)), ((), ()))
TN = (((0,), (0,)), ((), ()))
CROSS = (((0,), (1,)), ((), ()))


def mm(a, b, dims, out=f32):
    return lax.dot_general(a, b, dims, preferred_element_type=f32).astype(out)


def sigmoid(v):
    return 0.5 * jnp.tanh(0.5 * v) + 0.5


def seen(info, count):
    here = info[0:1, LANES : LANES + SPAN]
    return (info[0:1, LANES - count : LANES + SPAN - count] == here).astype(f32)


def shifts(info, row, sign):
    source = lax.broadcasted_iota(jnp.int32, (SPAN + LANES, SPAN), 0)
    target = lax.broadcasted_iota(jnp.int32, (SPAN + LANES, SPAN), 1)
    edge = 4 * row + 4 if sign == 1 else 4 * row - SPAN
    parts = []
    for k in range(1, TAPS):
        wanted = target - sign * k
        outside = wanted < 0 if sign == 1 else wanted >= SPAN
        wanted = jnp.where(outside, SPAN + edge + wanted, wanted)
        parts.append(jnp.where(source == wanted, seen(info, sign * k), 0.0).astype(bf16))
    return jnp.concatenate(parts, axis=1)


def twice(tile):
    return jnp.concatenate([tile, tile], axis=1)


def tap(taps, k):
    return jnp.broadcast_to(taps[:, k : k + 1], (taps.shape[0], SPAN))


def conv_kernel(
    raw_ref, halo_ref, info_ref, step_ref, log_ref, taps_ref, conv_ref, slope_ref, state_ref, wx_ref
):
    info = info_ref[0]
    before = shifts(info, pl.program_id(0), 1)
    here = info[0:1, LANES : LANES + SPAN]
    ending = (here == here[:, SPAN - 1 : SPAN]).astype(f32)
    logs = log_ref[...]
    weight = jnp.exp(logs[:, SPAN - 1 : SPAN] - logs) * step_ref[...] * ending
    heads = weight.shape[0]
    width = heads * HDIM
    for part in range(conv_ref.shape[0] // LANES):
        rows = pl.ds(part * LANES, LANES)
        raw = raw_ref[rows, :]
        shifted = mm(jnp.concatenate([raw, halo_ref[rows, :]], axis=1), before, NN)
        taps = taps_ref[rows, :]
        pre = tap(taps, TAPS) + tap(taps, 0) * raw.astype(f32)
        for k in range(1, TAPS):
            pre = pre + tap(taps, k) * shifted[:, (k - 1) * SPAN : k * SPAN]
        sig = sigmoid(pre)
        out = pre * sig
        conv_ref[rows, :] = out.astype(bf16)
        slope_ref[rows, :] = (sig + out * (1.0 - sig)).astype(bf16)
        if part * LANES < width:
            out = out.astype(bf16).astype(f32)
            for h in range(part * LANES // HDIM, (part + 1) * LANES // HDIM):
                at = h * HDIM - part * LANES
                scaled = out[at : at + HDIM] * weight[h : h + 1]
                wx_ref[pl.ds(h * HDIM, HDIM), :] = scaled.astype(bf16)
    keys = conv_ref[width : width + NSTATE, :]
    state_ref[0] = mm(wx_ref[...], keys, NT, bf16)


def link_bias(info, info_col):
    here = info[0:1, LANES : LANES + SPAN]
    u = lax.broadcasted_iota(jnp.int32, (SPAN, LANES), 0)
    t = lax.broadcasted_iota(jnp.int32, (SPAN, LANES), 1)
    same0 = info_col[:LANES] == here[:, :LANES]
    same1 = info_col == here[:, LANES:]
    first = jnp.where(jnp.logical_and(same0, u[:LANES] <= t[:LANES]), 0.0, -1e30)
    second = jnp.where(jnp.logical_and(same1, u <= t + LANES), 0.0, -1e30)
    return first, second


def within_kernel(conv_ref, info_ref, log_ref, shifted_ref, out_ref):
    info = info_ref[0]
    heads = log_ref.shape[0]
    width = heads * HDIM
    info_col = jnp.transpose(info[:, LANES : LANES + SPAN])[:, 0:1]
    bias0, bias1 = link_bias(info, info_col)
    keys = conv_ref[width : width + NSTATE, :]
    queries = conv_ref[width + NSTATE : width + 2 * NSTATE, :]
    score0 = mm(keys[:, :LANES], queries[:, :LANES], TN)
    score1 = mm(keys, queries[:, LANES:], TN)
    logs = log_ref[...]
    source = jnp.transpose(shifted_ref[...])
    for h in range(heads):
        rows = pl.ds(h * HDIM, HDIM)
        col = source[:, h : h + 1]
        m0 = jnp.exp(logs[h : h + 1, :LANES] - col[:LANES] + bias0) * score0
        m1 = jnp.exp(logs[h : h + 1, LANES:] - col + bias1) * score1
        x = conv_ref[rows, :]
        out_ref[rows, :LANES] = mm(x[:, :LANES], m0.astype(bf16), NN)
        out_ref[rows, LANES:] = mm(x, m1.astype(bf16), NN)


def carried_decay(info, logs):
    here = info[0:1, LANES : LANES + SPAN]
    carried = (here == info[0:1, LANES - 1 : LANES]).astype(f32)
    return jnp.exp(logs) * carried


def mix_kernel(
    conv_ref, info_ref, log_ref, state_ref, within_ref, gate_ref, grad_ref, skip_ref,
    gain_ref, mixed_ref, sums_ref,
):
    info = info_ref[0]
    heads = log_ref.shape[0]
    width = heads * HDIM
    decay = carried_decay(info, log_ref[...])
    fill = info[1:2, LANES : LANES + SPAN]
    queries = conv_ref[width + NSTATE : width + 2 * NSTATE, :]
    reading = mm(state_ref[0], queries, NN)
    square = jnp.zeros((HDIM, SPAN), f32)
    cross = jnp.zeros((HDIM, SPAN), f32)
    for h in range(heads):
        rows = pl.ds(h * HDIM, HDIM)
        x = conv_ref[rows, :].astype(f32)
        core = within_ref[rows, :] + decay[h : h + 1] * reading[h * HDIM : (h + 1) * HDIM]
        mixed = ((core + skip_ref[h : h + 1, 0:1] * x) * fill).astype(bf16)
        mixed_ref[rows, :] = mixed
        z = gate_ref[rows, :]
        gated = mixed.astype(f32) * (z * sigmoid(z))
        square = square + gated * gated
        cross = cross + gated * (grad_ref[rows, :] * twice(gain_ref[rows, :]))
    sums_ref[0:1, :] = jnp.sum(square, axis=0, keepdims=True)
    sums_ref[1:2, :] = jnp.sum(cross, axis=0, keepdims=True)
    sums_ref[2:8, :] = jnp.zeros((6, SPAN), f32)


def gate_kernel(
    matrix_ref, info_ref, log_ref, mixed_ref, gate_ref, grad_ref, sums_ref, gain_ref,
    hat_ref, dmixed_ref, dgate_ref, state_ref, ey_ref,
):
    info = info_ref[0]
    heads = log_ref.shape[0]
    decay = carried_decay(info, log_ref[...])
    fill = info[1:2, LANES : LANES + SPAN]
    inverse = lax.rsqrt(sums_ref[0:1, :] * (1.0 / DIN) + epsilon)
    along = inverse * inverse * sums_ref[1:2, :] * (1.0 / DIN)
    for h in range(heads):
        rows = pl.ds(h * HDIM, HDIM)
        z = gate_ref[rows, :]
        mixed = mixed_ref[rows, :].astype(f32)
        sig = sigmoid(z)
        silu = z * sig
        gated = mixed * silu
        gain = twice(gain_ref[rows, :])
        hat_ref[rows, :] = (gated * inverse * gain).astype(bf16)
        grad = inverse * (grad_ref[rows, :] * gain - gated * along)
        dgate_ref[rows, :] = (grad * mixed * (sig * (1.0 + z * (1.0 - sig)))).astype(bf16)
        dy = ((grad * silu).astype(bf16).astype(f32) * fill)
        dmixed_ref[rows, :] = dy.astype(bf16)
        ey_ref[rows, :] = (dy * decay[h : h + 1]).astype(bf16)
    queries = matrix_ref[NSTATE:, :]
    state_ref[0] = mm(ey_ref[...], queries, NT, bf16)


def within_back_kernel(
    conv_ref, info_ref, log_ref, shifted_ref, dy_ref, state_ref,
    dx_ref, dbc_ref, rows_ref, ey_ref, ds0_ref, ds1_ref,
):
    info = info_ref[0]
    heads = log_ref.shape[0]
    width = heads * HDIM
    info_col = jnp.transpose(info[:, LANES : LANES + SPAN])[:, 0:1]
    bias0, bias1 = link_bias(info, info_col)
    keys = conv_ref[width : width + NSTATE, :]
    queries = conv_ref[width + NSTATE : width + 2 * NSTATE, :]
    score0 = mm(keys[:, :LANES], queries[:, :LANES], TN)
    score1 = mm(keys, queries[:, LANES:], TN)
    logs = log_ref[...]
    source = jnp.transpose(shifted_ref[...])
    decay = carried_decay(info, logs)
    state = state_ref[0]
    reading = mm(state, queries, NN)
    for h in range(heads):
        rows = pl.ds(h * HDIM, HDIM)
        col = source[:, h : h + 1]
        d0 = jnp.exp(logs[h : h + 1, :LANES] - col[:LANES] + bias0)
        d1 = jnp.exp(logs[h : h + 1, LANES:] - col + bias1)
        m0 = (d0 * score0).astype(bf16)
        m1 = (d1 * score1).astype(bf16)
        x = conv_ref[rows, :]
        dy = dy_ref[rows, :]
        y0 = mm(x[:, :LANES], m0, NN)
        y1 = mm(x, m1, NN)
        dxa = mm(dy[:, :LANES], m0, NT)
        dxb = mm(dy[:, LANES:], m1, NT)
        g0 = mm(x[:, :LANES], dy[:, :LANES], TN) * d0
        g1 = mm(x, dy[:, LANES:], TN) * d1
        if h == 0:
            ds0_ref[...] = g0
            ds1_ref[...] = g1
        else:
            ds0_ref[...] += g0
            ds1_ref[...] += g1
        dx = jnp.concatenate([dxa + dxb[:, :LANES], dxb[:, LANES:]], axis=1)
        dx_ref[rows, :] = dx
        xf = x.astype(f32)
        dyf = dy.astype(f32)
        ey = dyf * decay[h : h + 1]
        ey_ref[rows, :] = ey.astype(bf16)
        inner = jnp.sum(xf * dx, axis=0, keepdims=True)
        y = jnp.concatenate([y0, y1], axis=1)
        across = reading[h * HDIM : (h + 1) * HDIM]
        outer = jnp.sum(dyf * y + ey * across, axis=0, keepdims=True)
        rows_ref[h : h + 1, :] = outer - inner
        rows_ref[heads + h : heads + h + 1, :] = inner
        rows_ref[2 * heads + h : 2 * heads + h + 1, :] = jnp.sum(dyf * xf, axis=0, keepdims=True)
    ds0 = ds0_ref[...].astype(bf16)
    ds1 = ds1_ref[...].astype(bf16)
    dkeys_b = mm(queries[:, LANES:], ds1, NT)
    dkeys_a = mm(queries[:, :LANES], ds0, NT)
    dbc_ref[:NSTATE, :LANES] = dkeys_a + dkeys_b[:, :LANES]
    dbc_ref[:NSTATE, LANES:] = dkeys_b[:, LANES:]
    dq_state = mm(state, ey_ref[...], TN)
    dbc_ref[NSTATE:, :LANES] = mm(keys[:, :LANES], ds0, NN) + dq_state[:, :LANES]
    dbc_ref[NSTATE:, LANES:] = mm(keys, ds1, NN) + dq_state[:, LANES:]


def state_back_kernel(
    conv_ref, slope_ref, info_ref, log_ref, step_ref, sig_ref, dy_ref, dx_ref, dbc_ref,
    rows_ref, dstate_ref, state_ref, par_ref,
    g_ref, dstep_ref, starts_ref, wx_ref,
):
    row = pl.program_id(0)
    info = info_ref[0]
    heads = log_ref.shape[0]
    width = heads * HDIM
    here = info[0:1, LANES : LANES + SPAN]
    ending = (here == here[:, SPAN - 1 : SPAN]).astype(f32)
    logs = log_ref[...]
    step = step_ref[...]
    last = logs[:, SPAN - 1 : SPAN]
    weight = jnp.exp(last - logs) * step * ending
    keep = jnp.exp(last) * (here[:, SPAN - 1 : SPAN] == info[0:1, LANES - 1 : LANES]).astype(f32)
    keys = conv_ref[width : width + NSTATE, :]
    dstate = dstate_ref[0]
    along = mm(dstate, keys, NN)
    inner_rows = []
    tail_rows = []
    for h in range(heads):
        rows = pl.ds(h * HDIM, HDIM)
        x = conv_ref[rows, :].astype(f32)
        w = weight[h : h + 1]
        wv = w * along[h * HDIM : (h + 1) * HDIM]
        wx_ref[rows, :] = (w * x).astype(bf16)
        inner_rows.append(jnp.sum(x * wv, axis=0, keepdims=True))
        product = dstate[h * HDIM : (h + 1) * HDIM].astype(f32) * state_ref[
            0, h * HDIM : (h + 1) * HDIM, :
        ].astype(f32)
        tail_rows.append(jnp.sum(jnp.sum(product, axis=0, keepdims=True), axis=1, keepdims=True))
        dx = dx_ref[rows, :] + wv + par_ref[h : h + 1, 0:1] * dy_ref[rows, :].astype(f32)
        g = dx * slope_ref[rows, :].astype(f32)
        g_ref[rows, :] = g.astype(bf16)

    inner = jnp.concatenate(inner_rows, axis=0)
    tail = jnp.concatenate(tail_rows, axis=0) * keep + jnp.sum(inner, axis=1, keepdims=True)
    dlog = rows_ref[0:heads, :] - inner
    t = lax.broadcasted_iota(jnp.int32, (SPAN, SPAN), 0)
    u = lax.broadcasted_iota(jnp.int32, (SPAN, SPAN), 1)
    later = (t >= u).astype(f32)
    dstepped = lax.dot_general(
        dlog, later, NN, precision=lax.Precision.HIGHEST, preferred_element_type=f32
    ) + tail
    rate = par_ref[:, 1:2]
    total = rows_ref[heads : 2 * heads, :] + inner
    sig = sig_ref[...]
    ratio = jnp.where(step > 1e-30, sig / jnp.maximum(step, 1e-30), 1.0)
    dstep_ref[0:heads, :] = total * ratio + rate * dstepped * sig
    dstep_ref[heads : 2 * heads, :] = dstepped * step * rate
    dkeys = dbc_ref[:NSTATE, :] + mm(dstate, wx_ref[...], TN)
    for start, grad in ((width, dkeys), (width + NSTATE, dbc_ref[NSTATE:, :])):
        rows = pl.ds(start, NSTATE)
        g_ref[rows, :] = (grad * slope_ref[rows, :].astype(f32)).astype(bf16)
    lane = lax.broadcasted_iota(jnp.int32, starts_ref.shape, 1)
    ours = jnp.logical_and(lane >= 4 * row, lane < 4 * row + 4)
    kept = jnp.where(row == 0, 0.0, starts_ref[...].astype(f32))
    fresh = pltpu.roll(g_ref[:, :LANES].astype(f32), 4 * row, 1)
    starts_ref[...] = jnp.where(ours, fresh, kept).astype(bf16)


def conv_back_kernel(
    raw_ref, halo_ref, g_ref, later_ref, info_ref, taps_ref, draw_ref, dtaps_ref
):
    row = pl.program_id(0)
    info = info_ref[0]
    before, after_ = shifts(info, row, 1), shifts(info, row, -1)
    size = min(LANES, raw_ref.shape[0])
    for part in range(raw_ref.shape[0] // size):
        rows = pl.ds(part * size, size)
        raw, low = raw_ref[rows, :], g_ref[rows, :]
        g = low.astype(f32)
        shifted = mm(jnp.concatenate([raw, halo_ref[rows, :]], axis=1), before, NN)
        ahead = mm(jnp.concatenate([low, later_ref[rows, :]], axis=1), after_, NN)
        taps = taps_ref[rows, :]
        draw = tap(taps, 0) * g
        products = [g * raw.astype(f32)]
        for k in range(1, TAPS):
            lanes = slice((k - 1) * SPAN, k * SPAN)
            draw = draw + tap(taps, k) * ahead[:, lanes]
            products.append(g * shifted[:, lanes])
        products.append(g)
        draw_ref[rows, :] = draw.astype(bf16)
        for k, product in enumerate(products):
            kept = jnp.where(row == 0, 0.0, dtaps_ref[k, rows, :])
            dtaps_ref[k, rows, :] = kept + product[:, :LANES] + product[:, LANES:]


def token_spec(channels):
    return pl.BlockSpec((channels, SPAN), lambda k, c: (0, k))


def part_spec(shape, start, by_token=False):
    lead = (0,) * (len(shape) - 2)
    return pl.BlockSpec(shape, lambda k, c: lead + (start(c), k if by_token else 0))


def fixed_spec(shape):
    return pl.BlockSpec(shape, lambda k, c: (0,) * len(shape))


def cell_spec(shape):
    return pl.BlockSpec((1,) + shape, lambda k, c: (k, 0, 0))


def call(kernel, rows, operands, in_specs, outs, out_specs, scratch=(), name=None, place=None):
    used = place is not None
    place = place if used else jnp.zeros((1,), jnp.int32)
    return pl.pallas_call(
        kernel if used else lambda place_ref, *refs: kernel(*refs),
        grid_spec=pltpu.PrefetchScalarGridSpec(
            num_scalar_prefetch=1,
            grid=(rows,),
            in_specs=in_specs,
            out_specs=out_specs,
            scratch_shapes=list(scratch),
        ),
        out_shape=outs,
        compiler_params=pltpu.CompilerParams(vmem_limit_bytes=50 * 1024 * 1024),
        cost_estimate=pl.CostEstimate(flops=0, bytes_accessed=0, transcendentals=0),
        name=name,
    )(place, *operands)


def finish_kernel(gate_ref, main_ref, tail_ref, weight_ref, grad_ref, sums_ref):
    total = jnp.zeros(sums_ref.shape, f32)
    ranks, _, width = gate_ref.shape
    matrix = slice(width, width + 2 * NSTATE)
    parts = [(gate_ref[q].astype(f32), q * width) for q in range(ranks)]
    parts += [(main_ref[q, :, :width].astype(f32), (ranks + q) * width) for q in range(ranks)]
    parts += [(sum(main_ref[q, :, matrix].astype(f32) for q in range(ranks)), 2 * ranks * width)]
    parts += [(tail_ref[...].astype(f32), 2 * ranks * width + 2 * NSTATE)]
    for value, start in parts:
        size = value.shape[1]
        grad_ref[:, start : start + size] = value
        product = value * weight_ref[:, start : start + size].astype(f32)
        whole = size // LANES * LANES
        for i in range(0, whole, LANES):
            total = total + product[:, i : i + LANES]
        if whole < size:
            rest = jnp.zeros((product.shape[0], LANES - size + whole), f32)
            total = total + jnp.concatenate([product[:, whole:], rest], axis=1)
    sums_ref[...] = total


def finish(gate_rows, main_rows, tail, weight):
    span_rows = weight.shape[0]
    return pl.pallas_call(
        finish_kernel,
        out_shape=[
            jax.ShapeDtypeStruct(weight.shape, f32),
            jax.ShapeDtypeStruct((span_rows, LANES), f32),
        ],
        compiler_params=pltpu.CompilerParams(vmem_limit_bytes=50 * 1024 * 1024),
        name="finish",
    )(gate_rows, main_rows, tail, weight)


def tie(*values):
    return lax.optimization_barrier(values)


def after(value, *others):
    return tie(value, *others)[0]


def shards(
    tokens, in_weight, norm_gain, out_weight, gate_gain, conv_weight, conv_bias, dt_bias, a_log,
    skip_gain, boundary, fill, cotangent,
):
    rows = lax.axis_size("row")
    head_axis = lax.axis_size("head")
    devices = rows * head_axis
    local, width_in = tokens.shape
    seq = boundary.shape[1]
    spans = seq // SPAN
    planes = spans // 2
    groups = head_axis // spans
    assert rows == 4 and local == SPAN and boundary.shape[0] == groups
    heads = HEADS // rows
    width = heads * HDIM
    span_rows = in_weight.shape[0]
    out_rows = out_weight.shape[0]
    count = rows * SPAN
    half = width_in // 2
    channels = width + 2 * NSTATE

    row = lax.axis_index("row")
    head = lax.axis_index("head")
    core = head % 2
    span = head % spans
    plane = span // 2
    group = head // spans
    first = core == 0

    def across_rows(a, mask):
        return lax.ppermute(a, "row", [(i, i ^ mask) for i in range(rows)])

    def over_heads(a, pairs):
        return lax.ppermute(a, "head", pairs)

    def device(g, p, c):
        return (g * planes + p) * 2 + c

    every = [(g, p, c) for g in range(groups) for p in range(planes) for c in range(2)]
    siblings = [(device(g, p, c), device(g, p, 1 - c)) for g, p, c in every]
    ring_up = [(device(g, p, c), device(g, (p + 1) % planes, c)) for g, p, c in every]
    ring_down = [(b, a) for a, b in ring_up]
    next_span = [(g * spans + b, g * spans + b + 1) for g in range(groups) for b in range(spans - 1)]
    last_span = [(b, a) for a, b in next_span]
    same_place = [
        [device(g, p, c) for g in range(groups)] for p in range(planes) for c in range(2)
    ]

    def hop_up(p):
        return [(device(g, p, c), device(g, p + 1, c)) for g in range(groups) for c in range(2)]

    def hop_down(p):
        return [(b, a) for a, b in hop_up(p)]

    def sibling(a):
        return over_heads(a, siblings)

    def by_core(zero, one):
        return jnp.where(first, zero, one)

    def all_rows(a):
        return lax.all_to_all(
            jnp.broadcast_to(a[None], (rows,) + a.shape), "row", 0, 0, tiled=True
        )

    def gather_groups(a):
        if groups == 1:
            return a
        return lax.all_gather(a, "head", axis=0, axis_index_groups=same_place, tiled=True)

    def everywhere(a):
        return lax.all_to_all(
            jnp.broadcast_to(a[None], (devices,) + a.shape), ("row", "head"), 0, 0, tiled=True
        )

    def arranged(a):
        whole = a.reshape(a.shape[0], rows, head_axis, span_rows)
        return whole.transpose(0, 2, 1, 3).reshape(a.shape[0], width_in)

    def restored(a):
        whole = a.reshape(a.shape[0], head_axis, rows, span_rows)
        return whole.transpose(0, 2, 1, 3).reshape(a.shape[0], width_in)

    def column_part(cols):
        return lax.all_to_all(cols, "row", 0, 0, tiled=True).reshape(rows * span_rows, -1)

    def place_parts(whole, pieces):
        size = pieces[0][0].shape[0]
        for i, both in enumerate(pieces):
            for e, part in enumerate(both):
                at = (plane - i) % planes * 2 + (core ^ e)
                if groups == 1:
                    found = [(at, part)]
                else:
                    every_group = lax.all_gather(
                        part, "head", axis=0, axis_index_groups=same_place
                    )
                    found = [(g * spans + at, every_group[g]) for g in range(groups)]
                for place, one in found:
                    whole = lax.dynamic_update_slice(whole, one, (place * size, 0))
        return whole

    def up_ring(a):
        return over_heads(a, ring_up)

    value_cols = in_weight[:, DIN : 2 * DIN].reshape(span_rows, rows, width).transpose(1, 0, 2)
    matrix_cols = in_weight[:, 2 * DIN : 2 * DIN + 2 * NSTATE]
    matrix_cols = jnp.broadcast_to(matrix_cols[None], (rows, span_rows, 2 * NSTATE))
    main = [column_part(jnp.concatenate([value_cols, matrix_cols], axis=2))]
    out_rank = lax.all_gather(out_weight, "head", axis=0, tiled=True)

    gains = jnp.stack(
        [jnp.pad(g.astype(f32), (0, LANES - g.shape[0])) for g in (norm_gain, gate_gain)]
    )
    gains = everywhere(after(jnp.pad(gains, ((0, 6), (0, 0))), main[0]))
    main.append(up_ring(main[0]))
    gains, main[1] = tie(gains, main[1])
    all_norm_gain = gains[:, 0, :span_rows].reshape(1, width_in)
    rank_gain = gains[:, 1, :out_rows].reshape(rows, width)
    rank_gain = lax.dynamic_index_in_dim(rank_gain, row, 0, keepdims=False)
    rank_gain = jnp.broadcast_to(rank_gain[:, None], (width, LANES))

    activations = tokens.astype(f32)
    inverse = lax.rsqrt(jnp.mean(activations * activations, axis=-1, keepdims=True) + epsilon)
    normed = activations * inverse
    projected_in = arranged((normed * all_norm_gain).astype(bf16))
    projected_in, main[1] = tie(projected_in, main[1])
    cut = SPAN // 2
    from_x, from_y = across_rows(projected_in, 1), across_rows(projected_in, 2)
    gate_cols = after(in_weight[:, :DIN], gains)
    gate_parts = [column_part(gate_cols.reshape(span_rows, rows, width).transpose(1, 0, 2))]
    for _ in range(planes - 2):
        main.append(up_ring(main[-1]))
    from_x, from_y, gate_parts[0], main[-1] = tie(from_x, from_y, gate_parts[0], main[-1])

    x_far, y_far = across_rows(from_x[:cut], 2), across_rows(from_y[cut:], 1)
    steps_cols = after(in_weight[:, 2 * DIN + 2 * NSTATE :], main[-1]).T
    steps_cols = steps_cols.reshape(rows, 1, heads, span_rows)
    steps_cols = jnp.broadcast_to(steps_cols, (rows, head_axis, heads, span_rows))
    steps_cols = lax.all_to_all(
        steps_cols.reshape(devices, heads, span_rows), ("row", "head"), 0, 0, tiled=True
    )
    step_weight = steps_cols.reshape(rows, head_axis, heads, span_rows).transpose(2, 1, 0, 3)
    step_weight = step_weight.reshape(heads, width_in)
    gate_parts.append(up_ring(gate_parts[0]))
    x_far, y_far, step_weight, gate_parts[1] = tie(x_far, y_far, step_weight, gate_parts[1])
    main_weight = jnp.zeros((width_in, channels + heads), bf16)
    main_weight = place_parts(main_weight, [(part, sibling(part)) for part in main])
    main_weight = lax.dynamic_update_slice(main_weight, step_weight.T, (0, channels))

    plane_in = jnp.zeros((count + LANES, width_in), bf16)
    ends_in = jnp.zeros((rows, 4, width_in), bf16)
    for part, source, start in (
        (projected_in, row, 0), (from_x, row ^ 1, 0), (from_y, row ^ 2, 0),
        (x_far, row ^ 3, 0), (y_far, row ^ 3, cut),
    ):
        plane_in = lax.dynamic_update_slice(plane_in, part, (source * SPAN + start, 0))
        if start + part.shape[0] == SPAN:
            ends_in = lax.dynamic_update_slice(ends_in, part[-4:][None], (source, 0, 0))
    halo_in = over_heads(ends_in.reshape(4 * rows, width_in), next_span)
    extended_in = lax.dynamic_update_slice(plane_in, halo_in, (count + 0 * row, 0))
    plane_in = extended_in[:count]

    segments = jnp.cumsum(boundary, axis=1).astype(f32)
    used = (jnp.arange(seq)[None, :] < fill[:, None]).astype(f32)
    says = jnp.stack(
        [
            jnp.pad(segments, ((0, 0), (LANES, LANES)), constant_values=-1.0),
            jnp.pad(used, ((0, 0), (LANES, LANES))),
        ],
        axis=1,
    )
    says = lax.dynamic_slice(says, (group, 0, span * SPAN), (1, 2, SPAN + 2 * LANES))[0]
    info = all_rows(after(jnp.pad(says, ((0, 6), (0, 0))), steps_cols))

    plane_cot = all_rows(after(cotangent, info)).reshape(count, width_in)

    local_step = lax.dynamic_slice_in_dim(dt_bias, row * heads, heads, 0)
    local_rate = -jnp.exp(lax.dynamic_slice_in_dim(a_log, row * heads, heads, 0))
    local_skip = lax.dynamic_slice_in_dim(skip_gain, row * heads, heads, 0)
    raw_steps = mm(step_weight, plane_in, NT, bf16).astype(f32)
    shifted_steps = raw_steps + local_step[:, None]
    steps = jax.nn.softplus(shifted_steps)
    step_slope = jax.nn.sigmoid(shifted_steps)
    earlier = jnp.triu(jnp.ones((SPAN, SPAN), f32))
    logs = lax.dot_general(
        (steps * local_rate[:, None]).reshape(heads * rows, SPAN), earlier, NN,
        precision=lax.Precision.HIGHEST, preferred_element_type=f32,
    ).reshape(heads, count)
    shifted_logs = logs - jnp.log(steps)
    params = jnp.pad(jnp.stack([local_skip, local_rate], axis=1), ((0, 0), (0, LANES - 2)))
    ends = logs.reshape(heads, rows, SPAN)[:, :, -1].T
    seg_ids = info[:, 0]
    unbroken = (seg_ids[:, LANES - 1] == seg_ids[:, LANES + SPAN - 1]).astype(f32)
    keep = jnp.exp(ends) * unbroken[:, None]
    keep_other = sibling(jnp.pad(keep, ((0, 0), (0, LANES - heads))))[:, :heads]
    keep, keep_other = keep[:, :, None, None], keep_other[:, :, None, None]
    keep_plane = keep * keep_other

    all_taps = jnp.concatenate([conv_weight, conv_bias[None]], axis=0)
    taps = jnp.concatenate(
        [lax.dynamic_slice_in_dim(all_taps, row * width, width, 1), all_taps[:, DIN:]], axis=1
    )
    taps = jnp.pad(taps.T, ((0, 0), (0, LANES - TAPS - 1)))

    raw = mm(main_weight[:, :channels], extended_in, CROSS, bf16)
    gate_parts.append(up_ring(gate_parts[1]))
    raw, gate_parts[2] = tie(raw, gate_parts[2])
    halo_spec = pl.BlockSpec((channels, LANES), lambda k, c: (0, count // LANES))
    shape = jax.ShapeDtypeStruct
    info_spec = cell_spec(info.shape[1:])
    state_spec = cell_spec((width, NSTATE))
    states = shape((rows, width, NSTATE), bf16)
    by_head = (rows, heads, HDIM, NSTATE)
    row_spec = token_spec(heads)
    wide = token_spec(width)
    tall = token_spec(channels)
    low_wide = shape((width, count), bf16)
    conv, slope, local_state = call(
        conv_kernel, rows, (raw, raw, info, steps, logs, taps),
        [tall, halo_spec, info_spec, row_spec, row_spec, fixed_spec(taps.shape)],
        [shape((channels, count), bf16), shape((channels, count), bf16), states],
        [tall, tall, state_spec],
        [pltpu.VMEM((width, SPAN), bf16)], name="conv",
    )

    for _ in range(planes - 3):
        gate_parts.append(up_ring(gate_parts[-1]))
    local_state, gate_parts[-1] = tie(local_state, gate_parts[-1])
    gate_weight = place_parts(
        jnp.zeros((width_in, width), bf16), [(part, sibling(part)) for part in gate_parts]
    )

    def pass_states(mine, hops, beside, near):
        other = sibling(mine)
        is_near = core == near

        def own_heads(a):
            return lax.dynamic_slice_in_dim(a, core * (heads // 2), heads // 2, 1).astype(f32)

        total = own_heads(jnp.where(is_near, other, mine)) + own_heads(
            jnp.where(is_near, keep_other, keep)
        ) * own_heads(jnp.where(is_near, mine, other))
        keep_half = own_heads(keep_plane)
        got = jnp.zeros((), f32)
        passed = []
        for hop, others in zip(hops, beside):
            running = after((total + keep_half * got).astype(bf16), *others)
            got = got + over_heads(running, hop).astype(f32)
            passed.append(got)
        got = got.astype(bf16)
        rest = sibling(got)
        whole = by_core(
            jnp.concatenate([got, rest], axis=1), jnp.concatenate([rest, got], axis=1)
        )
        through = (other.astype(f32) + keep_other * whole.astype(f32)).astype(bf16)
        return jnp.where(is_near, whole, through).reshape(states.shape), passed

    within = call(
        within_kernel, rows, (conv, info, logs, shifted_logs),
        [tall, info_spec, row_spec, row_spec],
        shape((width, count), f32), wide, name="within",
    )
    gate = mm(gate_weight, plane_in, CROSS)
    grad_hat = mm(out_rank, plane_cot, NT, bf16)

    state_in, _ = pass_states(
        local_state.reshape(by_head), [hop_up(p) for p in range(planes - 1)],
        [(), (within,), (gate, plane_cot)] + [()] * (planes - 4), 0,
    )

    mixed, sums = call(
        mix_kernel, rows, (conv, info, logs, state_in, within, gate, grad_hat, params, rank_gain),
        [tall, info_spec, row_spec, state_spec, wide, wide, wide, fixed_spec(params.shape),
         fixed_spec(rank_gain.shape)],
        [low_wide, shape((8, count), f32)], [wide, token_spec(8)], name="mix",
    )
    sums = sums + sum(across_rows(sums, m) for m in range(1, rows))

    gated_hat, dmixed, dgate, local_dstate = call(
        gate_kernel, rows, (conv, info, logs, mixed, gate, grad_hat, sums, rank_gain),
        [part_spec((2 * NSTATE, SPAN), lambda c: width // (2 * NSTATE), True), info_spec, row_spec,
         wide, wide, wide, token_spec(8), fixed_spec(rank_gain.shape)],
        [low_wide] * 3 + [states], [wide, wide, wide, state_spec],
        [pltpu.VMEM((width, SPAN), bf16)], name="gate",
    )

    def to_owner(partial_sum):
        got = lax.all_to_all(partial_sum.reshape(rows, SPAN, -1), "row", 0, 0, tiled=True)
        return jnp.sum(got.astype(f32), axis=0)

    def rows_product(grads):
        return mm(plane_in, grads, CROSS, bf16)

    def over_planes(product):
        return lax.psum_scatter(product, "head", scatter_dimension=0, tiled=True)

    def rows_to_owner(summed):
        return lax.all_to_all(summed.reshape(rows, span_rows, -1), "row", 0, 0, tiled=True)

    dgate_product = rows_product(dgate)
    dx, dmatrix, row_sums = call(
        within_back_kernel, rows, (conv, info, logs, shifted_logs, dmixed, state_in),
        [tall, info_spec, row_spec, row_spec, wide, state_spec],
        [shape((width, count), f32), shape((2 * NSTATE, count), f32), shape((3 * heads, count), f32)],
        [wide, token_spec(2 * NSTATE), token_spec(3 * heads)],
        [pltpu.VMEM((width, SPAN), bf16), pltpu.VMEM((LANES, LANES), f32),
         pltpu.VMEM((SPAN, LANES), f32)],
        name="within_back",
    )
    out_part = mm(gated_hat, out_rank, TN, bf16)
    dout = mm(gated_hat, plane_cot, NN, bf16)
    dstate_out, passed = pass_states(
        local_dstate.reshape(by_head), [hop_down(p) for p in reversed(range(planes - 1))],
        [(), (dgate_product, out_part), (dx,)] + [()] * (planes - 4), 1,
    )
    dgate_sum = over_planes(after(dgate_product, passed[1]))
    output = (activations + to_owner(out_part)).astype(bf16)
    gate_part = mm(dgate, gate_weight, CROSS, bf16)
    dstate_out = after(dstate_out, output, dout, gate_part)

    grad_conv, dsteps, grad_starts = call(
        state_back_kernel, rows,
        (conv, slope, info, logs, steps, step_slope, dmixed, dx, dmatrix, row_sums, dstate_out,
         state_in, params),
        [tall, tall, info_spec, row_spec, row_spec, row_spec, wide, wide, token_spec(2 * NSTATE),
         token_spec(3 * heads), state_spec, state_spec, fixed_spec(params.shape)],
        [shape((channels, count), bf16), shape((2 * heads, count), f32),
         shape((channels, LANES), bf16)],
        [tall, token_spec(2 * heads), fixed_spec((channels, LANES))],
        [pltpu.VMEM((width, SPAN), bf16)], name="state_back",
    )
    draw, dtaps = call(
        conv_back_kernel, rows,
        (raw, raw, grad_conv, over_heads(grad_starts, last_span), info, taps),
        [tall, halo_spec, tall, fixed_spec(grad_starts.shape), info_spec,
         fixed_spec(taps.shape)],
        [shape((channels, count), bf16), shape((TAPS + 1, channels, LANES), f32)],
        [tall, fixed_spec((TAPS + 1, channels, LANES))], name="conv_back",
    )

    dmain = jnp.concatenate([draw, dsteps[:heads].astype(bf16)], axis=0)
    dmain_product = rows_product(dmain)
    dmain_sum = over_planes(dmain_product)
    dgate_rows = rows_to_owner(dgate_sum)
    dmain_rows = rows_to_owner(after(dmain_sum, dgate_rows))
    dmain = after(dmain, dmain_product)
    grad_parts = []
    for lanes in (slice(0, half), slice(half, width_in)):
        part = mm(dmain, main_weight[lanes], CROSS) + gate_part[:, lanes].astype(f32)
        grad_parts.append(to_owner(part.astype(bf16)))
    grad_normed = restored(jnp.concatenate(grad_parts, axis=1)) * all_norm_gain
    grad_tokens = inverse * (
        grad_normed - normed * jnp.mean(grad_normed * normed, axis=-1, keepdims=True)
    )
    input_grad = (cotangent.astype(f32) + grad_tokens).astype(bf16)

    dout = after(dout, dgate_sum).reshape(groups, planes, 2, out_rows, width_in)
    dout_mine = by_core(dout[:, :, 0], dout[:, :, 1])
    dout_other = sibling(by_core(dout[:, :, 1], dout[:, :, 0]))

    def out_piece(i):
        at = (plane - i) % planes
        return sum(
            lax.dynamic_index_in_dim(a, at, 1, keepdims=False).astype(f32)
            for a in (dout_mine, dout_other)
        )

    running = out_piece(planes - 1)
    for i in reversed(range(planes - 1)):
        running = over_heads(running.astype(bf16), ring_down).astype(f32) + out_piece(i)
    if groups > 1:
        running = lax.psum_scatter(
            running, "head", scatter_dimension=0, axis_index_groups=same_place, tiled=True
        )
    out_weight_grad = running.reshape(out_rows, width_in)
    gate_gain_grad = jnp.sum(out_weight_grad * out_weight.astype(f32), axis=1) / gate_gain.astype(f32)

    tail = dmain_rows[..., channels:].transpose(1, 0, 2).reshape(span_rows, HEADS)
    in_weight_grad, norm_sums = finish(dgate_rows, dmain_rows, tail, in_weight)
    norm_gain_grad = jnp.sum(norm_sums, axis=1) / norm_gain.astype(f32)

    head_sums = jnp.sum(jnp.concatenate([dsteps, row_sums[2 * heads :]], axis=0), axis=1)
    taps_sum = jnp.sum(dtaps, axis=2)
    packed = after(jnp.concatenate([taps_sum.reshape(-1), head_sums]), *grad_parts)
    size = packed.shape[0]
    padded = -(-size // (8 * LANES)) * 8 * LANES
    packed = jnp.pad(packed, (0, padded - size)).reshape(padded // LANES, LANES)
    packed = jnp.broadcast_to(packed[None], (head_axis,) + packed.shape)
    packed = jnp.sum(lax.all_to_all(packed, "head", 0, 0, tiled=True), axis=0)
    total = all_rows(packed).reshape(rows, padded)
    taps_size = (TAPS + 1) * channels
    total_taps = total[:, :taps_size].reshape(rows, TAPS + 1, channels)
    all_taps_grad = jnp.concatenate(
        [
            total_taps[..., :width].transpose(1, 0, 2).reshape(TAPS + 1, DIN),
            jnp.sum(total_taps[..., width:], axis=0),
        ],
        axis=1,
    )
    total_heads = total[:, taps_size:size].reshape(rows, 3, heads)
    total_heads = total_heads.transpose(1, 0, 2).reshape(3, HEADS)
    return (
        output,
        input_grad,
        in_weight_grad,
        norm_gain_grad,
        out_weight_grad,
        gate_gain_grad,
        all_taps_grad[:TAPS],
        all_taps_grad[TAPS],
        total_heads[0],
        total_heads[1],
        total_heads[2],
    )


def solution(mesh):
    both = ("row", "head")
    return jax.shard_map(
        shards,
        mesh=mesh,
        in_specs=(
            P(both, None), P(both, None), P(both), P(both, None), P(both),
            P(), P(), P(), P(), P(),
            P("row", None), P("row"), P(both, None),
        ),
        out_specs=(
            P(both, None), P(both, None), P(both, None), P(both), P(both, None), P(both),
            P(), P(), P(), P(), P(),
        ),
        check_vma=False,
    )
```

```python
import jax
import jax.numpy as jnp
from jax import lax
from jax.experimental import pallas as pl
from jax.experimental.pallas import tpu as pltpu
from jax.sharding import PartitionSpec as P

HEADS = 64
HDIM = 64
NSTATE = 128
SPAN = 256
DIN = 4096
TAPS = 4
LANES = 128
epsilon = 1e-05

f32 = jnp.float32
bf16 = jnp.bfloat16

NN = (((1,), (0,)), ((), ()))
NT = (((1,), (1,)), ((), ()))
TN = (((0,), (0,)), ((), ()))
CROSS = (((0,), (1,)), ((), ()))


def mm(a, b, dims, out=f32):
    return lax.dot_general(a, b, dims, preferred_element_type=f32).astype(out)


def sigmoid(v):
    return 0.5 * jnp.tanh(0.5 * v) + 0.5


def seen(info, count):
    here = info[0:1, LANES : LANES + SPAN]
    return (info[0:1, LANES - count : LANES + SPAN - count] == here).astype(f32)


def shifts(info, row, sign):
    source = lax.broadcasted_iota(jnp.int32, (SPAN + LANES, SPAN), 0)
    target = lax.broadcasted_iota(jnp.int32, (SPAN + LANES, SPAN), 1)
    edge = 4 * row + 4 if sign == 1 else 4 * row - SPAN
    parts = []
    for k in range(1, TAPS):
        wanted = target - sign * k
        outside = wanted < 0 if sign == 1 else wanted >= SPAN
        wanted = jnp.where(outside, SPAN + edge + wanted, wanted)
        parts.append(jnp.where(source == wanted, seen(info, sign * k), 0.0).astype(bf16))
    return jnp.concatenate(parts, axis=1)


def twice(tile):
    return jnp.concatenate([tile, tile], axis=1)


def tap(taps, k):
    return jnp.broadcast_to(taps[:, k : k + 1], (taps.shape[0], SPAN))


def conv_kernel(
    raw_ref, halo_ref, info_ref, step_ref, log_ref, taps_ref, conv_ref, slope_ref, state_ref, wx_ref
):
    info = info_ref[0]
    before = shifts(info, pl.program_id(0), 1)
    here = info[0:1, LANES : LANES + SPAN]
    ending = (here == here[:, SPAN - 1 : SPAN]).astype(f32)
    logs = log_ref[...]
    weight = jnp.exp(logs[:, SPAN - 1 : SPAN] - logs) * step_ref[...] * ending
    heads = weight.shape[0]
    width = heads * HDIM
    for part in range(conv_ref.shape[0] // LANES):
        rows = pl.ds(part * LANES, LANES)
        raw = raw_ref[rows, :]
        shifted = mm(jnp.concatenate([raw, halo_ref[rows, :]], axis=1), before, NN)
        taps = taps_ref[rows, :]
        pre = tap(taps, TAPS) + tap(taps, 0) * raw.astype(f32)
        for k in range(1, TAPS):
            pre = pre + tap(taps, k) * shifted[:, (k - 1) * SPAN : k * SPAN]
        sig = sigmoid(pre)
        out = pre * sig
        conv_ref[rows, :] = out.astype(bf16)
        slope_ref[rows, :] = (sig + out * (1.0 - sig)).astype(bf16)
        if part * LANES < width:
            out = out.astype(bf16).astype(f32)
            for h in range(part * LANES // HDIM, (part + 1) * LANES // HDIM):
                at = h * HDIM - part * LANES
                scaled = out[at : at + HDIM] * weight[h : h + 1]
                wx_ref[pl.ds(h * HDIM, HDIM), :] = scaled.astype(bf16)
    keys = conv_ref[width : width + NSTATE, :]
    state_ref[0] = mm(wx_ref[...], keys, NT, bf16)


def link_bias(info, info_col):
    here = info[0:1, LANES : LANES + SPAN]
    u = lax.broadcasted_iota(jnp.int32, (SPAN, LANES), 0)
    t = lax.broadcasted_iota(jnp.int32, (SPAN, LANES), 1)
    same0 = info_col[:LANES] == here[:, :LANES]
    same1 = info_col == here[:, LANES:]
    first = jnp.where(jnp.logical_and(same0, u[:LANES] <= t[:LANES]), 0.0, -1e30)
    second = jnp.where(jnp.logical_and(same1, u <= t + LANES), 0.0, -1e30)
    return first, second


def within_kernel(conv_ref, info_ref, log_ref, shifted_ref, out_ref):
    info = info_ref[0]
    heads = log_ref.shape[0]
    width = heads * HDIM
    info_col = jnp.transpose(info[:, LANES : LANES + SPAN])[:, 0:1]
    bias0, bias1 = link_bias(info, info_col)
    keys = conv_ref[width : width + NSTATE, :]
    queries = conv_ref[width + NSTATE : width + 2 * NSTATE, :]
    score0 = mm(keys[:, :LANES], queries[:, :LANES], TN)
    score1 = mm(keys, queries[:, LANES:], TN)
    logs = log_ref[...]
    source = jnp.transpose(shifted_ref[...])
    for h in range(heads):
        rows = pl.ds(h * HDIM, HDIM)
        col = source[:, h : h + 1]
        m0 = jnp.exp(logs[h : h + 1, :LANES] - col[:LANES] + bias0) * score0
        m1 = jnp.exp(logs[h : h + 1, LANES:] - col + bias1) * score1
        x = conv_ref[rows, :]
        out_ref[rows, :LANES] = mm(x[:, :LANES], m0.astype(bf16), NN)
        out_ref[rows, LANES:] = mm(x, m1.astype(bf16), NN)


def carried_decay(info, logs):
    here = info[0:1, LANES : LANES + SPAN]
    carried = (here == info[0:1, LANES - 1 : LANES]).astype(f32)
    return jnp.exp(logs) * carried


def mix_kernel(
    conv_ref, info_ref, log_ref, state_ref, within_ref, gate_ref, grad_ref, skip_ref,
    gain_ref, mixed_ref, sums_ref,
):
    info = info_ref[0]
    heads = log_ref.shape[0]
    width = heads * HDIM
    decay = carried_decay(info, log_ref[...])
    fill = info[1:2, LANES : LANES + SPAN]
    queries = conv_ref[width + NSTATE : width + 2 * NSTATE, :]
    reading = mm(state_ref[0], queries, NN)
    square = jnp.zeros((HDIM, SPAN), f32)
    cross = jnp.zeros((HDIM, SPAN), f32)
    for h in range(heads):
        rows = pl.ds(h * HDIM, HDIM)
        x = conv_ref[rows, :].astype(f32)
        core = within_ref[rows, :] + decay[h : h + 1] * reading[h * HDIM : (h + 1) * HDIM]
        mixed = ((core + skip_ref[h : h + 1, 0:1] * x) * fill).astype(bf16)
        mixed_ref[rows, :] = mixed
        z = gate_ref[rows, :]
        gated = mixed.astype(f32) * (z * sigmoid(z))
        square = square + gated * gated
        cross = cross + gated * (grad_ref[rows, :] * twice(gain_ref[rows, :]))
    sums_ref[0:1, :] = jnp.sum(square, axis=0, keepdims=True)
    sums_ref[1:2, :] = jnp.sum(cross, axis=0, keepdims=True)
    sums_ref[2:8, :] = jnp.zeros((6, SPAN), f32)


def gate_kernel(
    matrix_ref, info_ref, log_ref, mixed_ref, gate_ref, grad_ref, sums_ref, gain_ref,
    hat_ref, dmixed_ref, dgate_ref, state_ref, ey_ref,
):
    info = info_ref[0]
    heads = log_ref.shape[0]
    decay = carried_decay(info, log_ref[...])
    fill = info[1:2, LANES : LANES + SPAN]
    inverse = lax.rsqrt(sums_ref[0:1, :] * (1.0 / DIN) + epsilon)
    along = inverse * inverse * sums_ref[1:2, :] * (1.0 / DIN)
    for h in range(heads):
        rows = pl.ds(h * HDIM, HDIM)
        z = gate_ref[rows, :]
        mixed = mixed_ref[rows, :].astype(f32)
        sig = sigmoid(z)
        silu = z * sig
        gated = mixed * silu
        gain = twice(gain_ref[rows, :])
        hat_ref[rows, :] = (gated * inverse * gain).astype(bf16)
        grad = inverse * (grad_ref[rows, :] * gain - gated * along)
        dgate_ref[rows, :] = (grad * mixed * (sig * (1.0 + z * (1.0 - sig)))).astype(bf16)
        dy = ((grad * silu).astype(bf16).astype(f32) * fill)
        dmixed_ref[rows, :] = dy.astype(bf16)
        ey_ref[rows, :] = (dy * decay[h : h + 1]).astype(bf16)
    queries = matrix_ref[NSTATE:, :]
    state_ref[0] = mm(ey_ref[...], queries, NT, bf16)


def within_back_kernel(
    conv_ref, info_ref, log_ref, shifted_ref, dy_ref, state_ref,
    dx_ref, dbc_ref, rows_ref, ey_ref, ds0_ref, ds1_ref,
):
    info = info_ref[0]
    heads = log_ref.shape[0]
    width = heads * HDIM
    info_col = jnp.transpose(info[:, LANES : LANES + SPAN])[:, 0:1]
    bias0, bias1 = link_bias(info, info_col)
    keys = conv_ref[width : width + NSTATE, :]
    queries = conv_ref[width + NSTATE : width + 2 * NSTATE, :]
    score0 = mm(keys[:, :LANES], queries[:, :LANES], TN)
    score1 = mm(keys, queries[:, LANES:], TN)
    logs = log_ref[...]
    source = jnp.transpose(shifted_ref[...])
    decay = carried_decay(info, logs)
    state = state_ref[0]
    reading = mm(state, queries, NN)
    for h in range(heads):
        rows = pl.ds(h * HDIM, HDIM)
        col = source[:, h : h + 1]
        d0 = jnp.exp(logs[h : h + 1, :LANES] - col[:LANES] + bias0)
        d1 = jnp.exp(logs[h : h + 1, LANES:] - col + bias1)
        m0 = (d0 * score0).astype(bf16)
        m1 = (d1 * score1).astype(bf16)
        x = conv_ref[rows, :]
        dy = dy_ref[rows, :]
        y0 = mm(x[:, :LANES], m0, NN)
        y1 = mm(x, m1, NN)
        dxa = mm(dy[:, :LANES], m0, NT)
        dxb = mm(dy[:, LANES:], m1, NT)
        g0 = mm(x[:, :LANES], dy[:, :LANES], TN) * d0
        g1 = mm(x, dy[:, LANES:], TN) * d1
        if h == 0:
            ds0_ref[...] = g0
            ds1_ref[...] = g1
        else:
            ds0_ref[...] += g0
            ds1_ref[...] += g1
        dx = jnp.concatenate([dxa + dxb[:, :LANES], dxb[:, LANES:]], axis=1)
        dx_ref[rows, :] = dx
        xf = x.astype(f32)
        dyf = dy.astype(f32)
        ey = dyf * decay[h : h + 1]
        ey_ref[rows, :] = ey.astype(bf16)
        inner = jnp.sum(xf * dx, axis=0, keepdims=True)
        y = jnp.concatenate([y0, y1], axis=1)
        across = reading[h * HDIM : (h + 1) * HDIM]
        outer = jnp.sum(dyf * y + ey * across, axis=0, keepdims=True)
        rows_ref[h : h + 1, :] = outer - inner
        rows_ref[heads + h : heads + h + 1, :] = inner
        rows_ref[2 * heads + h : 2 * heads + h + 1, :] = jnp.sum(dyf * xf, axis=0, keepdims=True)
    ds0 = ds0_ref[...].astype(bf16)
    ds1 = ds1_ref[...].astype(bf16)
    dkeys_b = mm(queries[:, LANES:], ds1, NT)
    dkeys_a = mm(queries[:, :LANES], ds0, NT)
    dbc_ref[:NSTATE, :LANES] = dkeys_a + dkeys_b[:, :LANES]
    dbc_ref[:NSTATE, LANES:] = dkeys_b[:, LANES:]
    dq_state = mm(state, ey_ref[...], TN)
    dbc_ref[NSTATE:, :LANES] = mm(keys[:, :LANES], ds0, NN) + dq_state[:, :LANES]
    dbc_ref[NSTATE:, LANES:] = mm(keys, ds1, NN) + dq_state[:, LANES:]


def state_back_kernel(
    conv_ref, slope_ref, info_ref, log_ref, step_ref, sig_ref, dy_ref, dx_ref, dbc_ref,
    rows_ref, dstate_ref, state_ref, par_ref,
    g_ref, dstep_ref, starts_ref, wx_ref,
):
    row = pl.program_id(0)
    info = info_ref[0]
    heads = log_ref.shape[0]
    width = heads * HDIM
    here = info[0:1, LANES : LANES + SPAN]
    ending = (here == here[:, SPAN - 1 : SPAN]).astype(f32)
    logs = log_ref[...]
    step = step_ref[...]
    last = logs[:, SPAN - 1 : SPAN]
    weight = jnp.exp(last - logs) * step * ending
    keep = jnp.exp(last) * (here[:, SPAN - 1 : SPAN] == info[0:1, LANES - 1 : LANES]).astype(f32)
    keys = conv_ref[width : width + NSTATE, :]
    dstate = dstate_ref[0]
    along = mm(dstate, keys, NN)
    inner_rows = []
    tail_rows = []
    for h in range(heads):
        rows = pl.ds(h * HDIM, HDIM)
        x = conv_ref[rows, :].astype(f32)
        w = weight[h : h + 1]
        wv = w * along[h * HDIM : (h + 1) * HDIM]
        wx_ref[rows, :] = (w * x).astype(bf16)
        inner_rows.append(jnp.sum(x * wv, axis=0, keepdims=True))
        product = dstate[h * HDIM : (h + 1) * HDIM].astype(f32) * state_ref[
            0, h * HDIM : (h + 1) * HDIM, :
        ].astype(f32)
        tail_rows.append(jnp.sum(jnp.sum(product, axis=0, keepdims=True), axis=1, keepdims=True))
        dx = dx_ref[rows, :] + wv + par_ref[h : h + 1, 0:1] * dy_ref[rows, :].astype(f32)
        g = dx * slope_ref[rows, :].astype(f32)
        g_ref[rows, :] = g.astype(bf16)

    inner = jnp.concatenate(inner_rows, axis=0)
    tail = jnp.concatenate(tail_rows, axis=0) * keep + jnp.sum(inner, axis=1, keepdims=True)
    dlog = rows_ref[0:heads, :] - inner
    t = lax.broadcasted_iota(jnp.int32, (SPAN, SPAN), 0)
    u = lax.broadcasted_iota(jnp.int32, (SPAN, SPAN), 1)
    later = (t >= u).astype(f32)
    dstepped = lax.dot_general(
        dlog, later, NN, precision=lax.Precision.HIGHEST, preferred_element_type=f32
    ) + tail
    rate = par_ref[:, 1:2]
    total = rows_ref[heads : 2 * heads, :] + inner
    sig = sig_ref[...]
    ratio = jnp.where(step > 1e-30, sig / jnp.maximum(step, 1e-30), 1.0)
    dstep_ref[0:heads, :] = total * ratio + rate * dstepped * sig
    dstep_ref[heads : 2 * heads, :] = dstepped * step * rate
    dkeys = dbc_ref[:NSTATE, :] + mm(dstate, wx_ref[...], TN)
    for start, grad in ((width, dkeys), (width + NSTATE, dbc_ref[NSTATE:, :])):
        rows = pl.ds(start, NSTATE)
        g_ref[rows, :] = (grad * slope_ref[rows, :].astype(f32)).astype(bf16)
    lane = lax.broadcasted_iota(jnp.int32, starts_ref.shape, 1)
    ours = jnp.logical_and(lane >= 4 * row, lane < 4 * row + 4)
    kept = jnp.where(row == 0, 0.0, starts_ref[...].astype(f32))
    fresh = pltpu.roll(g_ref[:, :LANES].astype(f32), 4 * row, 1)
    starts_ref[...] = jnp.where(ours, fresh, kept).astype(bf16)


def conv_back_kernel(
    raw_ref, halo_ref, g_ref, later_ref, info_ref, taps_ref, draw_ref, dtaps_ref
):
    row = pl.program_id(0)
    info = info_ref[0]
    before, after_ = shifts(info, row, 1), shifts(info, row, -1)
    size = min(LANES, raw_ref.shape[0])
    for part in range(raw_ref.shape[0] // size):
        rows = pl.ds(part * size, size)
        raw, low = raw_ref[rows, :], g_ref[rows, :]
        g = low.astype(f32)
        shifted = mm(jnp.concatenate([raw, halo_ref[rows, :]], axis=1), before, NN)
        ahead = mm(jnp.concatenate([low, later_ref[rows, :]], axis=1), after_, NN)
        taps = taps_ref[rows, :]
        draw = tap(taps, 0) * g
        products = [g * raw.astype(f32)]
        for k in range(1, TAPS):
            lanes = slice((k - 1) * SPAN, k * SPAN)
            draw = draw + tap(taps, k) * ahead[:, lanes]
            products.append(g * shifted[:, lanes])
        products.append(g)
        draw_ref[rows, :] = draw.astype(bf16)
        for k, product in enumerate(products):
            kept = jnp.where(row == 0, 0.0, dtaps_ref[k, rows, :])
            dtaps_ref[k, rows, :] = kept + product[:, :LANES] + product[:, LANES:]


def token_spec(channels):
    return pl.BlockSpec((channels, SPAN), lambda k, c: (0, k))


def part_spec(shape, start, by_token=False):
    lead = (0,) * (len(shape) - 2)
    return pl.BlockSpec(shape, lambda k, c: lead + (start(c), k if by_token else 0))


def fixed_spec(shape):
    return pl.BlockSpec(shape, lambda k, c: (0,) * len(shape))


def cell_spec(shape):
    return pl.BlockSpec((1,) + shape, lambda k, c: (k, 0, 0))


def call(kernel, rows, operands, in_specs, outs, out_specs, scratch=(), name=None, place=None):
    used = place is not None
    place = place if used else jnp.zeros((1,), jnp.int32)
    return pl.pallas_call(
        kernel if used else lambda place_ref, *refs: kernel(*refs),
        grid_spec=pltpu.PrefetchScalarGridSpec(
            num_scalar_prefetch=1,
            grid=(rows,),
            in_specs=in_specs,
            out_specs=out_specs,
            scratch_shapes=list(scratch),
        ),
        out_shape=outs,
        compiler_params=pltpu.CompilerParams(vmem_limit_bytes=50 * 1024 * 1024),
        cost_estimate=pl.CostEstimate(flops=0, bytes_accessed=0, transcendentals=0),
        name=name,
    )(place, *operands)


def finish_kernel(
    place_ref, *refs
):
    *gate_refs, main_ref, tail_ref, weight_ref, grad_ref, sums_ref = refs
    ranks, _, columns = main_ref.shape
    width = gate_refs[0].shape[1]
    matrix = slice(width, width + 2 * NSTATE)
    parts = [
        (ref[...].astype(f32), pl.multiple_of(jnp.bitwise_xor(place_ref[0], k) * width, LANES))
        for k, ref in enumerate(gate_refs)
    ]
    parts += [(main_ref[q, :, :width].astype(f32), (ranks + q) * width) for q in range(ranks)]
    parts += [(sum(main_ref[q, :, matrix].astype(f32) for q in range(ranks)), 2 * ranks * width)]
    parts += [(tail_ref[...].astype(f32), 2 * ranks * width + 2 * NSTATE)]
    total = jnp.zeros(sums_ref.shape, f32)
    for value, start in parts:
        size = value.shape[1]
        grad_ref[:, pl.ds(start, size)] = value
        product = value * weight_ref[:, pl.ds(start, size)].astype(f32)
        whole = size // LANES * LANES
        for i in range(0, whole, LANES):
            total = total + product[:, i : i + LANES]
        if whole < size:
            rest = jnp.zeros((product.shape[0], LANES - size + whole), f32)
            total = total + jnp.concatenate([product[:, whole:], rest], axis=1)
    sums_ref[...] = total


def finish(place, gate_rows, main_rows, tail, weight):
    operands = (*gate_rows, main_rows, tail, weight)
    outs = [
        jax.ShapeDtypeStruct(weight.shape, f32),
        jax.ShapeDtypeStruct((weight.shape[0], LANES), f32),
    ]
    return call(
        finish_kernel, 1, operands, [fixed_spec(a.shape) for a in operands],
        outs, [fixed_spec(o.shape) for o in outs], name="finish", place=place,
    )


def tie(*values):
    return lax.optimization_barrier(values)


class Clock:
    def __init__(self):
        self.last = ()

    def now(self, *values):
        out = tie(*values, *self.last)[: len(values)]
        return out if len(out) > 1 else out[0]

    def until(self, *values):
        self.last = values


def shards(
    tokens, in_weight, norm_gain, out_weight, gate_gain, conv_weight, conv_bias, dt_bias, a_log,
    skip_gain, boundary, fill, cotangent,
):
    rows = lax.axis_size("row")
    head_axis = lax.axis_size("head")
    devices = rows * head_axis
    local, width_in = tokens.shape
    seq = boundary.shape[1]
    spans = seq // SPAN
    planes = spans // 2
    groups = head_axis // spans
    assert rows == 4 and local == SPAN and boundary.shape[0] == groups
    heads = HEADS // rows
    width = heads * HDIM
    span_rows = in_weight.shape[0]
    out_rows = out_weight.shape[0]
    count = rows * SPAN
    half = width_in // 2
    channels = width + 2 * NSTATE

    row = lax.axis_index("row")
    head = lax.axis_index("head")
    core = head % 2
    span = head % spans
    plane = span // 2
    group = head // spans
    first = core == 0

    clock = Clock()
    now, until = clock.now, clock.until

    def across_rows(a, mask):
        return lax.ppermute(a, "row", [(i, i ^ mask) for i in range(rows)])

    def over_heads(a, pairs):
        return lax.ppermute(a, "head", pairs)

    def device(g, p, c):
        return (g * planes + p) * 2 + c

    every = [(g, p, c) for g in range(groups) for p in range(planes) for c in range(2)]
    siblings = [(device(g, p, c), device(g, p, 1 - c)) for g, p, c in every]
    ring_up = [(device(g, p, c), device(g, (p + 1) % planes, c)) for g, p, c in every]
    ring_down = [(b, a) for a, b in ring_up]
    next_span = [(g * spans + b, g * spans + b + 1) for g in range(groups) for b in range(spans - 1)]
    last_span = [(b, a) for a, b in next_span]
    same_place = [
        [device(g, p, c) for g in range(groups)] for p in range(planes) for c in range(2)
    ]

    def hop_up(p):
        return [(device(g, p, c), device(g, p + 1, c)) for g in range(groups) for c in range(2)]

    def hop_down(p):
        return [(b, a) for a, b in hop_up(p)]

    def sibling(a):
        return over_heads(a, siblings)

    def by_core(zero, one):
        return jnp.where(first, zero, one)

    def all_rows(a):
        return lax.all_to_all(
            jnp.broadcast_to(a[None], (rows,) + a.shape), "row", 0, 0, tiled=True
        )

    def gather_groups(a):
        if groups == 1:
            return a
        return lax.all_gather(a, "head", axis=0, axis_index_groups=same_place, tiled=True)

    def everywhere(a):
        return lax.all_to_all(
            jnp.broadcast_to(a[None], (devices,) + a.shape), ("row", "head"), 0, 0, tiled=True
        )

    def arranged(a):
        whole = a.reshape(a.shape[0], rows, head_axis, span_rows)
        return whole.transpose(0, 2, 1, 3).reshape(a.shape[0], width_in)

    def restored(a):
        whole = a.reshape(a.shape[0], head_axis, rows, span_rows)
        return whole.transpose(0, 2, 1, 3).reshape(a.shape[0], width_in)

    def column_part(cols):
        return lax.all_to_all(cols, "row", 0, 0, tiled=True).reshape(rows * span_rows, -1)

    def zeros(size, *since):
        zero = tie(jnp.zeros((), bf16), *since)[0]
        return jnp.broadcast_to(zero, size)

    def place_parts(whole, pieces, since=()):
        size = pieces[0][0].shape[0]
        for i, both in enumerate(pieces):
            if i < len(since):
                whole = tie(whole, since[i])[0]
            for e, part in enumerate(both):
                at = (plane - i) % planes * 2 + (core ^ e)
                if groups == 1:
                    found = [(at, part)]
                else:
                    every_group = lax.all_gather(
                        part, "head", axis=0, axis_index_groups=same_place
                    )
                    found = [(g * spans + at, every_group[g]) for g in range(groups)]
                for place, one in found:
                    whole = lax.dynamic_update_slice(whole, one, (place * size, 0))
        return whole

    def up_ring(a):
        return over_heads(a, ring_up)

    value_cols = in_weight[:, DIN : 2 * DIN].reshape(span_rows, rows, width).transpose(1, 0, 2)
    matrix_cols = in_weight[:, 2 * DIN : 2 * DIN + 2 * NSTATE]
    matrix_cols = jnp.broadcast_to(matrix_cols[None], (rows, span_rows, 2 * NSTATE))
    main = [column_part(jnp.concatenate([value_cols, matrix_cols], axis=2))]
    out_parts = [out_weight, up_ring(out_weight)]
    gate_cols = tie(in_weight[:, :DIN], main[0])[0]
    gate_parts = [column_part(gate_cols.reshape(span_rows, rows, width).transpose(1, 0, 2))]
    until(main[0], out_parts[1], gate_parts[0])

    segments = jnp.cumsum(boundary, axis=1)
    used = (jnp.arange(seq)[None, :] < fill[:, None]).astype(jnp.int32)
    edge = ((0, 0), (LANES, LANES))
    says = [
        jnp.pad(part, edge, constant_values=value)
        for part, value in ((segments // LANES, -1), (segments % LANES, 0), (used, 0))
    ]
    says = jnp.stack(says, axis=1).astype(bf16)
    reach = SPAN + 2 * LANES
    says = jnp.stack(
        [
            says[h // spans, :, h % spans * SPAN : h % spans * SPAN + reach]
            for h in range(head_axis)
        ]
    ).reshape(1, head_axis, -1, LANES)
    steps_cols = in_weight[:, 2 * DIN + 2 * NSTATE :].T.reshape(rows, 1, heads, span_rows)
    both_gains = [jnp.pad(g, (0, LANES - g.shape[0])) for g in (norm_gain, gate_gain)]
    table = [
        jnp.pad(steps_cols, ((0, 0), (0, 0), (0, 0), (0, LANES - span_rows))),
        jnp.stack(both_gains).reshape(1, 1, 2, LANES),
        says,
    ]
    table = jnp.concatenate(
        [jnp.broadcast_to(t, (rows, head_axis) + t.shape[2:]) for t in table], axis=2
    )
    table = jnp.pad(table, ((0, 0), (0, 0), (0, -table.shape[2] % 16), (0, 0)))
    table = now(table.reshape((devices,) + table.shape[2:]))
    table = lax.all_to_all(table, ("row", "head"), 0, 0, tiled=True)
    main.append(up_ring(now(main[0])))
    main_others = [sibling(now(main[0]))]
    until(table, main[1], main_others[0])
    table = table.reshape((rows, head_axis) + table.shape[1:])
    step_weight = table[:, :, :heads, :span_rows].transpose(2, 1, 0, 3).reshape(heads, width_in)
    all_norm_gain = table[:, :, heads, :span_rows].reshape(1, width_in).astype(f32)
    rank_gain = table[:, :, heads + 1, :out_rows].reshape(rows, width)
    rank_gain = lax.dynamic_index_in_dim(rank_gain, row, 0, keepdims=False).astype(f32)
    rank_gain = jnp.broadcast_to(rank_gain[:, None], (width, LANES))
    info = table[:, 0, heads + 2 : heads + 2 + 3 * reach // LANES].astype(f32)
    info = info.reshape(rows, 3, reach)
    info = jnp.stack([info[:, 0] * LANES + info[:, 1], info[:, 2]], axis=1)
    info = jnp.pad(info, ((0, 0), (0, 6), (0, 0)))

    activations = tokens.astype(f32)
    inverse = lax.rsqrt(jnp.mean(activations * activations, axis=-1, keepdims=True) + epsilon)
    normed = activations * inverse
    projected_in = arranged((normed * now(all_norm_gain)).astype(bf16))
    gain_arranged = arranged(all_norm_gain)
    main.append(up_ring(now(main[1])))
    main_others.append(sibling(now(main[1])))
    cut = SPAN // 2
    from_x, from_y = across_rows(projected_in, 1), across_rows(projected_in, 2)
    out_parts.append(up_ring(now(out_parts[1])))
    until(from_x, from_y, main[-1], main_others[-1], out_parts[-1])

    far_x, far_y = now(from_x[:cut], from_y[cut:])
    x_far, y_far = across_rows(far_x, 2), across_rows(far_y, 1)
    for _ in range(planes - 3):
        main_others.append(sibling(now(main[-1])))
        main.append(up_ring(now(main[-1])))
    until(x_far, y_far, main[-1], main_others[-1])
    main_others.append(sibling(now(main[-1])))
    main_weight = zeros((width_in, channels + heads), main[1])
    main_weight = place_parts(
        main_weight, list(zip(main, main_others)), [main[1], main[2]]
    )
    main_weight = lax.dynamic_update_slice(main_weight, step_weight.T, (0, channels))

    def of_plane(since, mine, x, y, far_of_x, far_of_y):
        whole = zeros((count, width_in), since)
        ends = jnp.zeros((rows, 4, width_in), bf16)
        for part, source, start in (
            (mine, row, 0), (x, row ^ 1, 0), (y, row ^ 2, 0),
            (far_of_x, row ^ 3, 0), (far_of_y, row ^ 3, cut),
        ):
            whole = lax.dynamic_update_slice(whole, part, (source * SPAN + start, 0))
            if start + part.shape[0] == SPAN:
                ends = lax.dynamic_update_slice(ends, part[-4:][None], (source, 0, 0))
        return whole, ends

    plane_in, ends_in = of_plane(main[2], projected_in, from_x, from_y, x_far, y_far)
    halo_in = over_heads(ends_in.reshape(4 * rows, width_in), next_span)
    gate_parts.append(up_ring(now(gate_parts[0])))
    cot_x, cot_y = across_rows(now(cotangent), 1), across_rows(now(cotangent), 2)

    local_step = lax.dynamic_slice_in_dim(dt_bias, row * heads, heads, 0)
    local_rate = -jnp.exp(lax.dynamic_slice_in_dim(a_log, row * heads, heads, 0))
    local_skip = lax.dynamic_slice_in_dim(skip_gain, row * heads, heads, 0)
    raw_steps = mm(step_weight, plane_in, NT, bf16).astype(f32)
    shifted_steps = raw_steps + local_step[:, None]
    steps = jax.nn.softplus(shifted_steps)
    step_slope = jax.nn.sigmoid(shifted_steps)
    earlier = jnp.triu(jnp.ones((SPAN, SPAN), f32))
    logs = lax.dot_general(
        (steps * local_rate[:, None]).reshape(heads * rows, SPAN), earlier, NN,
        precision=lax.Precision.HIGHEST, preferred_element_type=f32,
    ).reshape(heads, count)
    shifted_logs = logs - jnp.log(steps)
    params = jnp.pad(jnp.stack([local_skip, local_rate], axis=1), ((0, 0), (0, LANES - 2)))
    ends = logs.reshape(heads, rows, SPAN)[:, :, -1].T
    seg_ids = info[:, 0]
    unbroken = (seg_ids[:, LANES - 1] == seg_ids[:, LANES + SPAN - 1]).astype(f32)
    keep = jnp.exp(ends) * unbroken[:, None]
    keep_other = sibling(jnp.pad(keep, ((0, 0), (0, LANES - heads))))[:, :heads]
    keep, keep_other = keep[:, :, None, None], keep_other[:, :, None, None]
    keep_plane = keep * keep_other

    all_taps = jnp.concatenate([conv_weight, conv_bias[None]], axis=0)
    taps = jnp.concatenate(
        [lax.dynamic_slice_in_dim(all_taps, row * width, width, 1), all_taps[:, DIN:]], axis=1
    )
    taps = jnp.pad(taps.T, ((0, 0), (0, LANES - TAPS - 1)))

    raw = mm(main_weight[:, :channels], plane_in, CROSS, bf16)
    halo = mm(main_weight[:, :channels], halo_in, CROSS, bf16)
    until(raw, halo_in, gate_parts[1])
    gate_parts.append(up_ring(now(gate_parts[1])))
    halo_in = jnp.pad(now(halo_in), ((0, LANES - 4 * rows), (0, 0)))
    halo = mm(main_weight[:, :channels], halo_in, CROSS, bf16)
    shape = jax.ShapeDtypeStruct
    info_spec = cell_spec(info.shape[1:])
    state_spec = cell_spec((width, NSTATE))
    states = shape((rows, width, NSTATE), bf16)
    by_head = (rows, heads, HDIM, NSTATE)
    row_spec = token_spec(heads)
    wide = token_spec(width)
    tall = token_spec(channels)
    low_wide = shape((width, count), bf16)
    conv, slope, local_state = call(
        conv_kernel, rows, (raw, halo, info, steps, logs, taps),
        [tall, fixed_spec(halo.shape), info_spec, row_spec, row_spec, fixed_spec(taps.shape)],
        [shape((channels, count), bf16), shape((channels, count), bf16), states],
        [tall, tall, state_spec],
        [pltpu.VMEM((width, SPAN), bf16)], name="conv",
    )

    until(local_state, gate_parts[2], cot_x, cot_y)

    def pass_states(mine, hops, beside, near, other):
        is_near = core == near

        def own_heads(a):
            return lax.dynamic_slice_in_dim(a, core * (heads // 2), heads // 2, 1).astype(f32)

        total = own_heads(jnp.where(is_near, other, mine)) + own_heads(
            jnp.where(is_near, keep_other, keep)
        ) * own_heads(jnp.where(is_near, mine, other))
        keep_half = own_heads(keep_plane)
        got = jnp.zeros((), f32)
        for hop, step in zip(hops, beside):
            running = now((total + keep_half * got).astype(bf16))
            until(running)
            passed = over_heads(running, hop)
            until(passed, *step())
            got = got + passed.astype(f32)
        got = now(got.astype(bf16))
        rest = sibling(got)
        whole = by_core(
            jnp.concatenate([got, rest], axis=1), jnp.concatenate([rest, got], axis=1)
        )
        through = (other.astype(f32) + keep_other * whole.astype(f32)).astype(bf16)
        return jnp.where(is_near, whole, through).reshape(states.shape)

    seen = {}

    def within_step():
        seen["within"] = call(
            within_kernel, rows, (conv, info, logs, now(shifted_logs)),
            [tall, info_spec, row_spec, row_spec],
            shape((width, count), f32), wide, name="within",
        )
        for _ in range(planes - 3):
            gate_parts.append(up_ring(now(gate_parts[-1])))
        seen["far"] = across_rows(now(cot_x[:cut]), 2), across_rows(now(cot_y[cut:]), 1)
        return (seen["within"], gate_parts[-1]) + seen["far"]

    def gate_step():
        others = [sibling(now(part)) for part in gate_parts]
        gate_weight = place_parts(
            zeros((width_in, width), others[0]), list(zip(gate_parts, others))
        )
        seen["gate_weight"] = gate_weight
        seen["gate"] = mm(gate_weight, now(plane_in), CROSS)
        for _ in range(planes - 3):
            out_parts.append(up_ring(now(out_parts[-1])))
        return seen["gate"], out_parts[-1]

    def hat_step():
        far = now(*seen["far"])
        seen["cot"], _ = of_plane(far[0], cotangent, cot_x, cot_y, *far)
        out_others = [sibling(now(part)) for part in out_parts]
        seen["out_rank"] = place_parts(
            zeros((width, width_in), far[0]), list(zip(out_parts, out_others))
        )
        seen["hat"] = mm(seen["out_rank"], seen["cot"], NT, bf16)
        return (seen["hat"],)

    local_state = local_state.reshape(by_head)
    other_state = sibling(now(local_state))
    until(other_state)
    state_in = pass_states(
        local_state, [hop_up(p) for p in range(planes - 1)], [within_step, gate_step, hat_step], 0,
        other_state,
    )
    within, gate, grad_hat = seen["within"], seen["gate"], seen["hat"]
    gate_weight, plane_cot, out_rank = seen["gate_weight"], seen["cot"], seen["out_rank"]

    mixed, sums = call(
        mix_kernel, rows, (conv, info, logs, state_in, within, gate, grad_hat, params, rank_gain),
        [tall, info_spec, row_spec, state_spec, wide, wide, wide, fixed_spec(params.shape),
         fixed_spec(rank_gain.shape)],
        [low_wide, shape((8, count), f32)], [wide, token_spec(8)], name="mix",
    )
    sums = sums + sum(across_rows(sums, m) for m in range(1, rows))

    gated_hat, dmixed, dgate, local_dstate = call(
        gate_kernel, rows, (conv, info, logs, mixed, gate, grad_hat, sums, rank_gain),
        [part_spec((2 * NSTATE, SPAN), lambda c: width // (2 * NSTATE), True), info_spec, row_spec,
         wide, wide, wide, token_spec(8), fixed_spec(rank_gain.shape)],
        [low_wide] * 3 + [states], [wide, wide, wide, state_spec],
        [pltpu.VMEM((width, SPAN), bf16)], name="gate",
    )

    def to_owner(partial_sum):
        got = lax.all_to_all(partial_sum.reshape(rows, SPAN, -1), "row", 0, 0, tiled=True)
        return jnp.sum(got.astype(f32), axis=0)

    def rows_product(grads):
        return mm(plane_in, grads, CROSS, bf16)

    def over_planes(product):
        return lax.psum_scatter(product, "head", scatter_dimension=0, tiled=True)

    def dgate_step():
        seen["dgate"] = rows_product(now(dgate))
        out = mm(now(gated_hat), out_rank, TN, bf16)
        seen["out"] = lax.psum_scatter(out, "row", scatter_dimension=0, tiled=True)
        return seen["dgate"], out

    def within_back_step():
        seen["back"] = call(
            within_back_kernel, rows, (conv, info, logs, shifted_logs, now(dmixed), state_in),
            [tall, info_spec, row_spec, row_spec, wide, state_spec],
            [shape((width, count), f32), shape((2 * NSTATE, count), f32),
             shape((3 * heads, count), f32)],
            [wide, token_spec(2 * NSTATE), token_spec(3 * heads)],
            [pltpu.VMEM((width, SPAN), bf16), pltpu.VMEM((LANES, LANES), f32),
             pltpu.VMEM((SPAN, LANES), f32)],
            name="within_back",
        )
        return seen["back"][:1]

    def out_step():
        seen["dgate_sum"] = over_planes(now(seen["dgate"]))
        seen["dout"] = mm(now(gated_hat), plane_cot, NN, bf16)
        seen["gate_part"] = mm(now(dgate), gate_weight, CROSS, bf16)
        seen["own"] = arranged(now(normed)), arranged(now(cotangent))
        return (seen["dout"], seen["gate_part"]) + seen["own"]

    local_dstate = local_dstate.reshape(by_head)
    other_dstate = sibling(local_dstate)
    until(other_dstate)
    dstate_out = pass_states(
        local_dstate, [hop_down(p) for p in reversed(range(planes - 1))],
        [dgate_step, within_back_step, out_step], 1, other_dstate,
    )
    dx, dmatrix, row_sums = seen["back"]
    output = (activations + seen["out"].astype(f32)).astype(bf16)

    grad_conv, dsteps, grad_starts = call(
        state_back_kernel, rows,
        (conv, slope, info, logs, steps, step_slope, dmixed, dx, dmatrix, row_sums, dstate_out,
         state_in, params),
        [tall, tall, info_spec, row_spec, row_spec, row_spec, wide, wide, token_spec(2 * NSTATE),
         token_spec(3 * heads), state_spec, state_spec, fixed_spec(params.shape)],
        [shape((channels, count), bf16), shape((2 * heads, count), f32),
         shape((channels, LANES), bf16)],
        [tall, token_spec(2 * heads), fixed_spec((channels, LANES))],
        [pltpu.VMEM((width, SPAN), bf16)], name="state_back",
    )
    until(grad_starts)

    dout = now(seen["dout"]).reshape(groups, planes, 2, out_rows, width_in)
    dout_mine = by_core(dout[:, :, 0], dout[:, :, 1])
    dout_other = sibling(by_core(dout[:, :, 1], dout[:, :, 0]))
    next_starts = over_heads(now(grad_starts), last_span)
    until(next_starts, dout_other)

    def out_piece(i):
        at = (plane - i) % planes
        return sum(
            lax.dynamic_index_in_dim(a, at, 1, keepdims=False).astype(f32)
            for a in (dout_mine, dout_other)
        )

    def head_exchange(dtaps):
        taps_sum = jnp.sum(dtaps, axis=2).reshape(-1)
        head_sums = jnp.sum(jnp.concatenate([dsteps, row_sums[2 * heads :]], axis=0), axis=1)
        packed = jnp.concatenate([taps_sum, head_sums])
        padded = -(-packed.shape[0] // (8 * LANES)) * 8 * LANES
        packed = jnp.pad(packed, (0, padded - packed.shape[0])).reshape(padded // LANES, LANES)
        packed = jnp.broadcast_to(packed[None], (head_axis,) + packed.shape)
        return lax.all_to_all(packed, "head", 0, 0, tiled=True)

    def conv_back_step():
        seen["draw"], seen["dtaps"] = call(
            conv_back_kernel, rows, (raw, halo, now(grad_conv), next_starts, info, taps),
            [tall, fixed_spec(halo.shape), tall, fixed_spec(grad_starts.shape), info_spec,
             fixed_spec(taps.shape)],
            [shape((channels, count), bf16), shape((TAPS + 1, channels, LANES), f32)],
            [tall, fixed_spec((TAPS + 1, channels, LANES))], name="conv_back",
        )
        return (seen["draw"],)

    def second_half_step():
        got = to_owner(seen["part"])
        seen["part"] = grad_part(1)
        return got, seen["part"]

    def last_step():
        got = to_owner(now(seen["part"]))
        seen["others"] = [across_rows(now(params), m) for m in range(1, rows)]
        return [got] + seen["others"]

    def grad_part(i):
        lanes = slice(i * half, (i + 1) * half)
        part = mm(now(seen["dmain"]), main_weight[lanes], CROSS)
        return (part + seen["gate_part"][:, lanes].astype(f32)).astype(bf16)

    grad_parts = []
    running = out_piece(planes - 1)
    for i, step in zip(
        reversed(range(planes - 1)), (conv_back_step, second_half_step, last_step)
    ):
        passed = over_heads(now(running.astype(bf16)), ring_down)
        found = step()
        until(passed, *found)
        running = passed.astype(f32) + out_piece(i)
        if step is not conv_back_step:
            grad_parts.append(found[0])
            continue
        dmain = jnp.concatenate([now(seen["draw"]), dsteps[:heads].astype(bf16)], axis=0)
        product = rows_product(dmain)
        dmain_sum = over_planes(tie(product, seen["dgate_sum"])[0])
        params = head_exchange(now(seen["dtaps"]))
        until(product, params)
        seen["dmain"] = dmain
        seen["part"] = grad_part(0)
        sums = now(seen["dgate_sum"]).reshape(rows, span_rows, -1)
        gate_rows = [
            lax.dynamic_index_in_dim(sums, row ^ m, 0, keepdims=False) for m in range(rows)
        ]
        gate_rows[1:] = [across_rows(part, m) for m, part in enumerate(gate_rows) if m]
        params = jnp.sum(now(params), axis=0)
        until(seen["part"], *gate_rows)
        seen["part"] = now(seen["part"])
    if groups > 1:
        running = lax.psum_scatter(
            running, "head", scatter_dimension=0, axis_index_groups=same_place, tiled=True
        )
    out_weight_grad = running.reshape(out_rows, width_in)
    gate_gain_grad = jnp.sum(out_weight_grad * out_weight.astype(f32), axis=1) / gate_gain.astype(f32)

    dmain_rows = lax.all_to_all(dmain_sum.reshape(rows, span_rows, -1), "row", 0, 0, tiled=True)
    every = jnp.zeros((rows, params.size), f32)
    for m, part in enumerate([params] + seen["others"]):
        every = lax.dynamic_update_slice(every, part.reshape(1, -1), (row ^ m, 0))
    total = every

    normed_arranged, cot_arranged = seen["own"]
    grad_normed = jnp.concatenate(grad_parts, axis=1) * gain_arranged
    grad_tokens = inverse * (
        grad_normed
        - normed_arranged * jnp.mean(grad_normed * normed_arranged, axis=-1, keepdims=True)
    )
    input_grad = restored((cot_arranged.astype(f32) + grad_tokens).astype(bf16))

    tail = dmain_rows[..., channels:].transpose(1, 0, 2).reshape(span_rows, HEADS)
    place = jnp.reshape(row, (1,)).astype(jnp.int32)
    in_weight_grad, norm_sums = finish(place, gate_rows, dmain_rows, tail, in_weight)
    norm_gain_grad = jnp.sum(norm_sums, axis=1) / norm_gain.astype(f32)

    taps_size, size = (TAPS + 1) * channels, (TAPS + 1) * channels + 3 * heads
    total_taps = total[:, :taps_size].reshape(rows, TAPS + 1, channels)
    all_taps_grad = jnp.concatenate(
        [
            total_taps[..., :width].transpose(1, 0, 2).reshape(TAPS + 1, DIN),
            jnp.sum(total_taps[..., width:], axis=0),
        ],
        axis=1,
    )
    total_heads = total[:, taps_size:size].reshape(rows, 3, heads)
    total_heads = total_heads.transpose(1, 0, 2).reshape(3, HEADS)
    return (
        output,
        input_grad,
        in_weight_grad,
        norm_gain_grad,
        out_weight_grad,
        gate_gain_grad,
        all_taps_grad[:TAPS],
        all_taps_grad[TAPS],
        total_heads[0],
        total_heads[1],
        total_heads[2],
    )


def solution(mesh):
    both = ("row", "head")
    return jax.shard_map(
        shards,
        mesh=mesh,
        in_specs=(
            P(both, None), P(both, None), P(both), P(both, None), P(both),
            P(), P(), P(), P(), P(),
            P("row", None), P("row"), P(both, None),
        ),
        out_specs=(
            P(both, None), P(both, None), P(both, None), P(both), P(both, None), P(both),
            P(), P(), P(), P(), P(),
        ),
        check_vma=False,
    )
```

```python
import jax
import jax.numpy as jnp
from jax import lax
from jax.experimental import pallas as pl
from jax.experimental.pallas import tpu as pltpu
from jax.sharding import PartitionSpec as P

HEADS = 64
HDIM = 64
NSTATE = 128
SPAN = 256
DIN = 4096
TAPS = 4
LANES = 128
epsilon = 1e-05

f32 = jnp.float32
bf16 = jnp.bfloat16

NN = (((1,), (0,)), ((), ()))
NT = (((1,), (1,)), ((), ()))
TN = (((0,), (0,)), ((), ()))
CROSS = (((0,), (1,)), ((), ()))


def mm(a, b, dims, out=f32):
    return lax.dot_general(a, b, dims, preferred_element_type=f32).astype(out)


def sigmoid(v):
    return 0.5 * jnp.tanh(0.5 * v) + 0.5


def seen(info, count):
    here = info[0:1, LANES : LANES + SPAN]
    return (info[0:1, LANES - count : LANES + SPAN - count] == here).astype(f32)


def shifts(info, row, sign):
    source = lax.broadcasted_iota(jnp.int32, (SPAN + LANES, SPAN), 0)
    target = lax.broadcasted_iota(jnp.int32, (SPAN + LANES, SPAN), 1)
    edge = 4 * row + 4 if sign == 1 else 4 * row - SPAN
    parts = []
    for k in range(1, TAPS):
        wanted = target - sign * k
        outside = wanted < 0 if sign == 1 else wanted >= SPAN
        wanted = jnp.where(outside, SPAN + edge + wanted, wanted)
        parts.append(jnp.where(source == wanted, seen(info, sign * k), 0.0).astype(bf16))
    return jnp.concatenate(parts, axis=1)


def twice(tile):
    return jnp.concatenate([tile, tile], axis=1)


def tap(taps, k):
    return jnp.broadcast_to(taps[:, k : k + 1], (taps.shape[0], SPAN))


def conv_kernel(
    raw_ref, halo_ref, info_ref, step_ref, log_ref, taps_ref, conv_ref, slope_ref, state_ref, wx_ref
):
    info = info_ref[0]
    before = shifts(info, pl.program_id(0), 1)
    here = info[0:1, LANES : LANES + SPAN]
    ending = (here == here[:, SPAN - 1 : SPAN]).astype(f32)
    logs = log_ref[...]
    weight = jnp.exp(logs[:, SPAN - 1 : SPAN] - logs) * step_ref[...] * ending
    heads = weight.shape[0]
    width = heads * HDIM
    for part in range(conv_ref.shape[0] // LANES):
        rows = pl.ds(part * LANES, LANES)
        raw = raw_ref[rows, :]
        shifted = mm(jnp.concatenate([raw, halo_ref[rows, :]], axis=1), before, NN)
        taps = taps_ref[rows, :]
        pre = tap(taps, TAPS) + tap(taps, 0) * raw.astype(f32)
        for k in range(1, TAPS):
            pre = pre + tap(taps, k) * shifted[:, (k - 1) * SPAN : k * SPAN]
        sig = sigmoid(pre)
        out = pre * sig
        conv_ref[rows, :] = out.astype(bf16)
        slope_ref[rows, :] = (sig + out * (1.0 - sig)).astype(bf16)
        if part * LANES < width:
            out = out.astype(bf16).astype(f32)
            for h in range(part * LANES // HDIM, (part + 1) * LANES // HDIM):
                at = h * HDIM - part * LANES
                scaled = out[at : at + HDIM] * weight[h : h + 1]
                wx_ref[pl.ds(h * HDIM, HDIM), :] = scaled.astype(bf16)
    keys = conv_ref[width : width + NSTATE, :]
    state_ref[0] = mm(wx_ref[...], keys, NT, bf16)


def link_bias(info, info_col):
    here = info[0:1, LANES : LANES + SPAN]
    u = lax.broadcasted_iota(jnp.int32, (SPAN, LANES), 0)
    t = lax.broadcasted_iota(jnp.int32, (SPAN, LANES), 1)
    same0 = info_col[:LANES] == here[:, :LANES]
    same1 = info_col == here[:, LANES:]
    first = jnp.where(jnp.logical_and(same0, u[:LANES] <= t[:LANES]), 0.0, -1e30)
    second = jnp.where(jnp.logical_and(same1, u <= t + LANES), 0.0, -1e30)
    return first, second


def within_kernel(conv_ref, info_ref, log_ref, shifted_ref, out_ref):
    info = info_ref[0]
    heads = log_ref.shape[0]
    width = heads * HDIM
    info_col = jnp.transpose(info[:, LANES : LANES + SPAN])[:, 0:1]
    bias0, bias1 = link_bias(info, info_col)
    keys = conv_ref[width : width + NSTATE, :]
    queries = conv_ref[width + NSTATE : width + 2 * NSTATE, :]
    score0 = mm(keys[:, :LANES], queries[:, :LANES], TN)
    score1 = mm(keys, queries[:, LANES:], TN)
    logs = log_ref[...]
    source = jnp.transpose(shifted_ref[...])
    for h in range(heads):
        rows = pl.ds(h * HDIM, HDIM)
        col = source[:, h : h + 1]
        m0 = jnp.exp(logs[h : h + 1, :LANES] - col[:LANES] + bias0) * score0
        m1 = jnp.exp(logs[h : h + 1, LANES:] - col + bias1) * score1
        x = conv_ref[rows, :]
        out_ref[rows, :LANES] = mm(x[:, :LANES], m0.astype(bf16), NN)
        out_ref[rows, LANES:] = mm(x, m1.astype(bf16), NN)


def carried_decay(info, logs):
    here = info[0:1, LANES : LANES + SPAN]
    carried = (here == info[0:1, LANES - 1 : LANES]).astype(f32)
    return jnp.exp(logs) * carried


def mix_kernel(
    conv_ref, info_ref, log_ref, state_ref, within_ref, gate_ref, grad_ref, skip_ref,
    gain_ref, mixed_ref, sums_ref,
):
    info = info_ref[0]
    heads = log_ref.shape[0]
    width = heads * HDIM
    decay = carried_decay(info, log_ref[...])
    fill = info[1:2, LANES : LANES + SPAN]
    queries = conv_ref[width + NSTATE : width + 2 * NSTATE, :]
    reading = mm(state_ref[0], queries, NN)
    square = jnp.zeros((HDIM, SPAN), f32)
    cross = jnp.zeros((HDIM, SPAN), f32)
    for h in range(heads):
        rows = pl.ds(h * HDIM, HDIM)
        x = conv_ref[rows, :].astype(f32)
        core = within_ref[rows, :] + decay[h : h + 1] * reading[h * HDIM : (h + 1) * HDIM]
        mixed = ((core + skip_ref[h : h + 1, 0:1] * x) * fill).astype(bf16)
        mixed_ref[rows, :] = mixed
        z = gate_ref[rows, :]
        gated = mixed.astype(f32) * (z * sigmoid(z))
        square = square + gated * gated
        cross = cross + gated * (grad_ref[rows, :] * twice(gain_ref[rows, :]))
    sums_ref[0:1, :] = jnp.sum(square, axis=0, keepdims=True)
    sums_ref[1:2, :] = jnp.sum(cross, axis=0, keepdims=True)
    sums_ref[2:8, :] = jnp.zeros((6, SPAN), f32)


def gate_kernel(
    matrix_ref, info_ref, log_ref, mixed_ref, gate_ref, grad_ref, sums_ref, gain_ref,
    hat_ref, dmixed_ref, dgate_ref, state_ref, ey_ref,
):
    info = info_ref[0]
    heads = log_ref.shape[0]
    decay = carried_decay(info, log_ref[...])
    fill = info[1:2, LANES : LANES + SPAN]
    inverse = lax.rsqrt(sums_ref[0:1, :] * (1.0 / DIN) + epsilon)
    along = inverse * inverse * sums_ref[1:2, :] * (1.0 / DIN)
    for h in range(heads):
        rows = pl.ds(h * HDIM, HDIM)
        z = gate_ref[rows, :]
        mixed = mixed_ref[rows, :].astype(f32)
        sig = sigmoid(z)
        silu = z * sig
        gated = mixed * silu
        gain = twice(gain_ref[rows, :])
        hat_ref[rows, :] = (gated * inverse * gain).astype(bf16)
        grad = inverse * (grad_ref[rows, :] * gain - gated * along)
        dgate_ref[rows, :] = (grad * mixed * (sig * (1.0 + z * (1.0 - sig)))).astype(bf16)
        dy = ((grad * silu).astype(bf16).astype(f32) * fill)
        dmixed_ref[rows, :] = dy.astype(bf16)
        ey_ref[rows, :] = (dy * decay[h : h + 1]).astype(bf16)
    queries = matrix_ref[NSTATE:, :]
    state_ref[0] = mm(ey_ref[...], queries, NT, bf16)


def within_back_kernel(
    conv_ref, info_ref, log_ref, shifted_ref, dy_ref, state_ref,
    dx_ref, dbc_ref, rows_ref, ey_ref, ds0_ref, ds1_ref,
):
    info = info_ref[0]
    heads = log_ref.shape[0]
    width = heads * HDIM
    info_col = jnp.transpose(info[:, LANES : LANES + SPAN])[:, 0:1]
    bias0, bias1 = link_bias(info, info_col)
    keys = conv_ref[width : width + NSTATE, :]
    queries = conv_ref[width + NSTATE : width + 2 * NSTATE, :]
    score0 = mm(keys[:, :LANES], queries[:, :LANES], TN)
    score1 = mm(keys, queries[:, LANES:], TN)
    logs = log_ref[...]
    source = jnp.transpose(shifted_ref[...])
    decay = carried_decay(info, logs)
    state = state_ref[0]
    reading = mm(state, queries, NN)
    for h in range(heads):
        rows = pl.ds(h * HDIM, HDIM)
        col = source[:, h : h + 1]
        d0 = jnp.exp(logs[h : h + 1, :LANES] - col[:LANES] + bias0)
        d1 = jnp.exp(logs[h : h + 1, LANES:] - col + bias1)
        m0 = (d0 * score0).astype(bf16)
        m1 = (d1 * score1).astype(bf16)
        x = conv_ref[rows, :]
        dy = dy_ref[rows, :]
        y0 = mm(x[:, :LANES], m0, NN)
        y1 = mm(x, m1, NN)
        dxa = mm(dy[:, :LANES], m0, NT)
        dxb = mm(dy[:, LANES:], m1, NT)
        g0 = mm(x[:, :LANES], dy[:, :LANES], TN) * d0
        g1 = mm(x, dy[:, LANES:], TN) * d1
        if h == 0:
            ds0_ref[...] = g0
            ds1_ref[...] = g1
        else:
            ds0_ref[...] += g0
            ds1_ref[...] += g1
        dx = jnp.concatenate([dxa + dxb[:, :LANES], dxb[:, LANES:]], axis=1)
        dx_ref[rows, :] = dx
        xf = x.astype(f32)
        dyf = dy.astype(f32)
        ey = dyf * decay[h : h + 1]
        ey_ref[rows, :] = ey.astype(bf16)
        inner = jnp.sum(xf * dx, axis=0, keepdims=True)
        y = jnp.concatenate([y0, y1], axis=1)
        across = reading[h * HDIM : (h + 1) * HDIM]
        outer = jnp.sum(dyf * y + ey * across, axis=0, keepdims=True)
        rows_ref[h : h + 1, :] = outer - inner
        rows_ref[heads + h : heads + h + 1, :] = inner
        rows_ref[2 * heads + h : 2 * heads + h + 1, :] = jnp.sum(dyf * xf, axis=0, keepdims=True)
    ds0 = ds0_ref[...].astype(bf16)
    ds1 = ds1_ref[...].astype(bf16)
    dkeys_b = mm(queries[:, LANES:], ds1, NT)
    dkeys_a = mm(queries[:, :LANES], ds0, NT)
    dbc_ref[:NSTATE, :LANES] = dkeys_a + dkeys_b[:, :LANES]
    dbc_ref[:NSTATE, LANES:] = dkeys_b[:, LANES:]
    dq_state = mm(state, ey_ref[...], TN)
    dbc_ref[NSTATE:, :LANES] = mm(keys[:, :LANES], ds0, NN) + dq_state[:, :LANES]
    dbc_ref[NSTATE:, LANES:] = mm(keys, ds1, NN) + dq_state[:, LANES:]


def state_back_kernel(
    conv_ref, slope_ref, info_ref, log_ref, step_ref, sig_ref, dy_ref, dx_ref, dbc_ref,
    rows_ref, dstate_ref, state_ref, par_ref,
    g_ref, dstep_ref, starts_ref, wx_ref,
):
    row = pl.program_id(0)
    info = info_ref[0]
    heads = log_ref.shape[0]
    width = heads * HDIM
    here = info[0:1, LANES : LANES + SPAN]
    ending = (here == here[:, SPAN - 1 : SPAN]).astype(f32)
    logs = log_ref[...]
    step = step_ref[...]
    last = logs[:, SPAN - 1 : SPAN]
    weight = jnp.exp(last - logs) * step * ending
    keep = jnp.exp(last) * (here[:, SPAN - 1 : SPAN] == info[0:1, LANES - 1 : LANES]).astype(f32)
    keys = conv_ref[width : width + NSTATE, :]
    dstate = dstate_ref[0]
    along = mm(dstate, keys, NN)
    inner_rows = []
    tail_rows = []
    for h in range(heads):
        rows = pl.ds(h * HDIM, HDIM)
        x = conv_ref[rows, :].astype(f32)
        w = weight[h : h + 1]
        wv = w * along[h * HDIM : (h + 1) * HDIM]
        wx_ref[rows, :] = (w * x).astype(bf16)
        inner_rows.append(jnp.sum(x * wv, axis=0, keepdims=True))
        product = dstate[h * HDIM : (h + 1) * HDIM].astype(f32) * state_ref[
            0, h * HDIM : (h + 1) * HDIM, :
        ].astype(f32)
        tail_rows.append(jnp.sum(jnp.sum(product, axis=0, keepdims=True), axis=1, keepdims=True))
        dx = dx_ref[rows, :] + wv + par_ref[h : h + 1, 0:1] * dy_ref[rows, :].astype(f32)
        g = dx * slope_ref[rows, :].astype(f32)
        g_ref[rows, :] = g.astype(bf16)

    inner = jnp.concatenate(inner_rows, axis=0)
    tail = jnp.concatenate(tail_rows, axis=0) * keep + jnp.sum(inner, axis=1, keepdims=True)
    dlog = rows_ref[0:heads, :] - inner
    t = lax.broadcasted_iota(jnp.int32, (SPAN, SPAN), 0)
    u = lax.broadcasted_iota(jnp.int32, (SPAN, SPAN), 1)
    later = (t >= u).astype(f32)
    dstepped = lax.dot_general(
        dlog, later, NN, precision=lax.Precision.HIGHEST, preferred_element_type=f32
    ) + tail
    rate = par_ref[:, 1:2]
    total = rows_ref[heads : 2 * heads, :] + inner
    sig = sig_ref[...]
    ratio = jnp.where(step > 1e-30, sig / jnp.maximum(step, 1e-30), 1.0)
    dstep_ref[0:heads, :] = total * ratio + rate * dstepped * sig
    dstep_ref[heads : 2 * heads, :] = dstepped * step * rate
    dkeys = dbc_ref[:NSTATE, :] + mm(dstate, wx_ref[...], TN)
    for start, grad in ((width, dkeys), (width + NSTATE, dbc_ref[NSTATE:, :])):
        rows = pl.ds(start, NSTATE)
        g_ref[rows, :] = (grad * slope_ref[rows, :].astype(f32)).astype(bf16)
    lane = lax.broadcasted_iota(jnp.int32, starts_ref.shape, 1)
    ours = jnp.logical_and(lane >= 4 * row, lane < 4 * row + 4)
    kept = jnp.where(row == 0, 0.0, starts_ref[...].astype(f32))
    fresh = pltpu.roll(g_ref[:, :LANES].astype(f32), 4 * row, 1)
    starts_ref[...] = jnp.where(ours, fresh, kept).astype(bf16)


def conv_back_kernel(
    raw_ref, halo_ref, g_ref, later_ref, info_ref, taps_ref, draw_ref, dtaps_ref
):
    row = pl.program_id(0)
    info = info_ref[0]
    before, after_ = shifts(info, row, 1), shifts(info, row, -1)
    size = min(LANES, raw_ref.shape[0])
    for part in range(raw_ref.shape[0] // size):
        rows = pl.ds(part * size, size)
        raw, low = raw_ref[rows, :], g_ref[rows, :]
        g = low.astype(f32)
        shifted = mm(jnp.concatenate([raw, halo_ref[rows, :]], axis=1), before, NN)
        ahead = mm(jnp.concatenate([low, later_ref[rows, :]], axis=1), after_, NN)
        taps = taps_ref[rows, :]
        draw = tap(taps, 0) * g
        products = [g * raw.astype(f32)]
        for k in range(1, TAPS):
            lanes = slice((k - 1) * SPAN, k * SPAN)
            draw = draw + tap(taps, k) * ahead[:, lanes]
            products.append(g * shifted[:, lanes])
        products.append(g)
        draw_ref[rows, :] = draw.astype(bf16)
        for k, product in enumerate(products):
            kept = jnp.where(row == 0, 0.0, dtaps_ref[k, rows, :])
            dtaps_ref[k, rows, :] = kept + product[:, :LANES] + product[:, LANES:]


def token_spec(channels):
    return pl.BlockSpec((channels, SPAN), lambda k, c: (0, k))


def part_spec(shape, start, by_token=False):
    lead = (0,) * (len(shape) - 2)
    return pl.BlockSpec(shape, lambda k, c: lead + (start(c), k if by_token else 0))


def fixed_spec(shape):
    return pl.BlockSpec(shape, lambda k, c: (0,) * len(shape))


def cell_spec(shape):
    return pl.BlockSpec((1,) + shape, lambda k, c: (k, 0, 0))


def call(kernel, rows, operands, in_specs, outs, out_specs, scratch=(), name=None, place=None):
    used = place is not None
    place = place if used else jnp.zeros((1,), jnp.int32)
    return pl.pallas_call(
        kernel if used else lambda place_ref, *refs: kernel(*refs),
        grid_spec=pltpu.PrefetchScalarGridSpec(
            num_scalar_prefetch=1,
            grid=(rows,),
            in_specs=in_specs,
            out_specs=out_specs,
            scratch_shapes=list(scratch),
        ),
        out_shape=outs,
        compiler_params=pltpu.CompilerParams(vmem_limit_bytes=50 * 1024 * 1024),
        cost_estimate=pl.CostEstimate(flops=0, bytes_accessed=0, transcendentals=0),
        name=name,
    )(place, *operands)


def finish_kernel(
    place_ref, *refs
):
    *gate_refs, main_ref, tail_ref, weight_ref, grad_ref, sums_ref = refs
    ranks, _, columns = main_ref.shape
    width = gate_refs[0].shape[1]
    matrix = slice(width, width + 2 * NSTATE)
    parts = [
        (ref[...].astype(f32), pl.multiple_of(jnp.bitwise_xor(place_ref[0], k) * width, LANES))
        for k, ref in enumerate(gate_refs)
    ]
    parts += [(main_ref[q, :, :width].astype(f32), (ranks + q) * width) for q in range(ranks)]
    parts += [(sum(main_ref[q, :, matrix].astype(f32) for q in range(ranks)), 2 * ranks * width)]
    parts += [(tail_ref[...].astype(f32), 2 * ranks * width + 2 * NSTATE)]
    total = jnp.zeros(sums_ref.shape, f32)
    for value, start in parts:
        size = value.shape[1]
        grad_ref[:, pl.ds(start, size)] = value
        product = value * weight_ref[:, pl.ds(start, size)].astype(f32)
        whole = size // LANES * LANES
        for i in range(0, whole, LANES):
            total = total + product[:, i : i + LANES]
        if whole < size:
            rest = jnp.zeros((product.shape[0], LANES - size + whole), f32)
            total = total + jnp.concatenate([product[:, whole:], rest], axis=1)
    sums_ref[...] = total


def finish(place, gate_rows, main_rows, tail, weight):
    operands = (*gate_rows, main_rows, tail, weight)
    outs = [
        jax.ShapeDtypeStruct(weight.shape, f32),
        jax.ShapeDtypeStruct((weight.shape[0], LANES), f32),
    ]
    return call(
        finish_kernel, 1, operands, [fixed_spec(a.shape) for a in operands],
        outs, [fixed_spec(o.shape) for o in outs], name="finish", place=place,
    )


def tie(*values):
    return lax.optimization_barrier(values)


class Clock:
    def __init__(self):
        self.last = ()

    def now(self, *values):
        out = tie(*values, *self.last)[: len(values)]
        return out if len(out) > 1 else out[0]

    def until(self, *values):
        self.last = values


def shards(
    tokens, in_weight, norm_gain, out_weight, gate_gain, conv_weight, conv_bias, dt_bias, a_log,
    skip_gain, boundary, fill, cotangent,
):
    rows = lax.axis_size("row")
    head_axis = lax.axis_size("head")
    devices = rows * head_axis
    local, width_in = tokens.shape
    seq = boundary.shape[1]
    spans = seq // SPAN
    planes = spans // 2
    groups = head_axis // spans
    assert rows == 4 and local == SPAN and boundary.shape[0] == groups
    heads = HEADS // rows
    width = heads * HDIM
    span_rows = in_weight.shape[0]
    out_rows = out_weight.shape[0]
    count = rows * SPAN
    half = width_in // 2
    channels = width + 2 * NSTATE

    row = lax.axis_index("row")
    head = lax.axis_index("head")
    core = head % 2
    span = head % spans
    plane = span // 2
    group = head // spans
    first = core == 0

    clock = Clock()
    now, until = clock.now, clock.until

    def across_rows(a, mask):
        return lax.ppermute(a, "row", [(i, i ^ mask) for i in range(rows)])

    def over_heads(a, pairs):
        return lax.ppermute(a, "head", pairs)

    def device(g, p, c):
        return (g * planes + p) * 2 + c

    every = [(g, p, c) for g in range(groups) for p in range(planes) for c in range(2)]
    siblings = [(device(g, p, c), device(g, p, 1 - c)) for g, p, c in every]
    ring_up = [(device(g, p, c), device(g, (p + 1) % planes, c)) for g, p, c in every]
    ring_down = [(b, a) for a, b in ring_up]
    next_span = [(g * spans + b, g * spans + b + 1) for g in range(groups) for b in range(spans - 1)]
    last_span = [(b, a) for a, b in next_span]
    same_place = [
        [device(g, p, c) for g in range(groups)] for p in range(planes) for c in range(2)
    ]

    def hop_up(p):
        return [(device(g, p, c), device(g, p + 1, c)) for g in range(groups) for c in range(2)]

    def hop_down(p):
        return [(b, a) for a, b in hop_up(p)]

    def sibling(a):
        return over_heads(a, siblings)

    def by_core(zero, one):
        return jnp.where(first, zero, one)

    def all_rows(a):
        return lax.all_to_all(
            jnp.broadcast_to(a[None], (rows,) + a.shape), "row", 0, 0, tiled=True
        )

    def gather_groups(a):
        if groups == 1:
            return a
        return lax.all_gather(a, "head", axis=0, axis_index_groups=same_place, tiled=True)

    def everywhere(a):
        return lax.all_to_all(
            jnp.broadcast_to(a[None], (devices,) + a.shape), ("row", "head"), 0, 0, tiled=True
        )

    def arranged(a):
        whole = a.reshape(a.shape[0], rows, head_axis, span_rows)
        return whole.transpose(0, 2, 1, 3).reshape(a.shape[0], width_in)

    def restored(a):
        whole = a.reshape(a.shape[0], head_axis, rows, span_rows)
        return whole.transpose(0, 2, 1, 3).reshape(a.shape[0], width_in)

    def column_part(cols):
        return lax.all_to_all(cols, "row", 0, 0, tiled=True).reshape(rows * span_rows, -1)

    def zeros(size, *since):
        zero = tie(jnp.zeros((), bf16), *since)[0]
        return jnp.broadcast_to(zero, size)

    def place_parts(whole, pieces, since=()):
        size = pieces[0][0].shape[0]
        for i, both in enumerate(pieces):
            if i < len(since):
                whole = tie(whole, since[i])[0]
            for e, part in enumerate(both):
                at = (plane - i) % planes * 2 + (core ^ e)
                if groups == 1:
                    found = [(at, part)]
                else:
                    every_group = lax.all_gather(
                        part, "head", axis=0, axis_index_groups=same_place
                    )
                    found = [(g * spans + at, every_group[g]) for g in range(groups)]
                for place, one in found:
                    whole = lax.dynamic_update_slice(whole, one, (place * size, 0))
        return whole

    def up_ring(a):
        return over_heads(a, ring_up)

    value_cols = in_weight[:, DIN : 2 * DIN].reshape(span_rows, rows, width).transpose(1, 0, 2)
    matrix_cols = in_weight[:, 2 * DIN : 2 * DIN + 2 * NSTATE]
    matrix_cols = jnp.broadcast_to(matrix_cols[None], (rows, span_rows, 2 * NSTATE))
    main = [column_part(jnp.concatenate([value_cols, matrix_cols], axis=2))]
    out_parts = [out_weight, up_ring(out_weight)]
    gate_cols = tie(in_weight[:, :DIN], main[0])[0]
    gate_parts = [column_part(gate_cols.reshape(span_rows, rows, width).transpose(1, 0, 2))]
    until(main[0], out_parts[1], gate_parts[0])

    segments = jnp.cumsum(boundary, axis=1)
    used = (jnp.arange(seq)[None, :] < fill[:, None]).astype(jnp.int32)
    edge = ((0, 0), (LANES, LANES))
    says = [
        jnp.pad(part, edge, constant_values=value)
        for part, value in ((segments // LANES, -1), (segments % LANES, 0), (used, 0))
    ]
    says = jnp.stack(says, axis=1).astype(bf16)
    reach = SPAN + 2 * LANES
    says = jnp.stack(
        [
            says[h // spans, :, h % spans * SPAN : h % spans * SPAN + reach]
            for h in range(head_axis)
        ]
    ).reshape(1, head_axis, -1, LANES)
    steps_cols = in_weight[:, 2 * DIN + 2 * NSTATE :].T.reshape(rows, 1, heads, span_rows)
    both_gains = [jnp.pad(g, (0, LANES - g.shape[0])) for g in (norm_gain, gate_gain)]
    table = [
        jnp.pad(steps_cols, ((0, 0), (0, 0), (0, 0), (0, LANES - span_rows))),
        jnp.stack(both_gains).reshape(1, 1, 2, LANES),
        says,
    ]
    table = jnp.concatenate(
        [jnp.broadcast_to(t, (rows, head_axis) + t.shape[2:]) for t in table], axis=2
    )
    table = jnp.pad(table, ((0, 0), (0, 0), (0, -table.shape[2] % 16), (0, 0)))
    table = now(table.reshape((devices,) + table.shape[2:]))
    table = lax.all_to_all(table, ("row", "head"), 0, 0, tiled=True)
    main.append(up_ring(now(main[0])))
    main_others = [sibling(now(main[0]))]
    until(table, main[1], main_others[0])
    table = table.reshape((rows, head_axis) + table.shape[1:])
    step_weight = table[:, :, :heads, :span_rows].transpose(2, 1, 0, 3).reshape(heads, width_in)
    all_norm_gain = table[:, :, heads, :span_rows].reshape(1, width_in).astype(f32)
    rank_gain = table[:, :, heads + 1, :out_rows].reshape(rows, width)
    rank_gain = lax.dynamic_index_in_dim(rank_gain, row, 0, keepdims=False).astype(f32)
    rank_gain = jnp.broadcast_to(rank_gain[:, None], (width, LANES))
    info = table[:, 0, heads + 2 : heads + 2 + 3 * reach // LANES].astype(f32)
    info = info.reshape(rows, 3, reach)
    info = jnp.stack([info[:, 0] * LANES + info[:, 1], info[:, 2]], axis=1)
    info = jnp.pad(info, ((0, 0), (0, 6), (0, 0)))

    activations = tokens.astype(f32)
    inverse = lax.rsqrt(jnp.mean(activations * activations, axis=-1, keepdims=True) + epsilon)
    normed = activations * inverse
    projected_in = arranged((normed * now(all_norm_gain)).astype(bf16))
    gain_arranged = arranged(all_norm_gain)
    main.append(up_ring(now(main[1])))
    main_others.append(sibling(now(main[1])))
    cut = SPAN // 2
    from_x, from_y = across_rows(projected_in, 1), across_rows(projected_in, 2)
    out_parts.append(up_ring(now(out_parts[1])))
    until(from_x, from_y, main[-1], main_others[-1], out_parts[-1])

    far_x, far_y = now(from_x[:cut], from_y[cut:])
    x_far, y_far = across_rows(far_x, 2), across_rows(far_y, 1)
    for _ in range(planes - 3):
        main_others.append(sibling(now(main[-1])))
        main.append(up_ring(now(main[-1])))
    until(x_far, y_far, main[-1], main_others[-1])
    main_others.append(sibling(now(main[-1])))
    main_weight = zeros((width_in, channels + heads), main[1])
    main_weight = place_parts(
        main_weight, list(zip(main, main_others)), [main[1], main[2]]
    )
    main_weight = lax.dynamic_update_slice(main_weight, step_weight.T, (0, channels))

    def of_plane(since, mine, x, y, far_of_x, far_of_y):
        whole = zeros((count, width_in), since)
        ends = jnp.zeros((rows, 4, width_in), bf16)
        for part, source, start in (
            (mine, row, 0), (x, row ^ 1, 0), (y, row ^ 2, 0),
            (far_of_x, row ^ 3, 0), (far_of_y, row ^ 3, cut),
        ):
            whole = lax.dynamic_update_slice(whole, part, (source * SPAN + start, 0))
            if start + part.shape[0] == SPAN:
                ends = lax.dynamic_update_slice(ends, part[-4:][None], (source, 0, 0))
        return whole, ends

    plane_in, ends_in = of_plane(main[2], projected_in, from_x, from_y, x_far, y_far)
    halo_in = over_heads(ends_in.reshape(4 * rows, width_in), next_span)
    gate_parts.append(up_ring(now(gate_parts[0])))
    cot_x, cot_y = across_rows(now(cotangent), 1), across_rows(now(cotangent), 2)

    local_step = lax.dynamic_slice_in_dim(dt_bias, row * heads, heads, 0)
    local_rate = -jnp.exp(lax.dynamic_slice_in_dim(a_log, row * heads, heads, 0))
    local_skip = lax.dynamic_slice_in_dim(skip_gain, row * heads, heads, 0)
    raw_steps = mm(step_weight, plane_in, NT, bf16).astype(f32)
    shifted_steps = raw_steps + local_step[:, None]
    steps = jax.nn.softplus(shifted_steps)
    step_slope = jax.nn.sigmoid(shifted_steps)
    earlier = jnp.triu(jnp.ones((SPAN, SPAN), f32))
    logs = lax.dot_general(
        (steps * local_rate[:, None]).reshape(heads * rows, SPAN), earlier, NN,
        precision=lax.Precision.HIGHEST, preferred_element_type=f32,
    ).reshape(heads, count)
    shifted_logs = logs - jnp.log(steps)
    params = jnp.pad(jnp.stack([local_skip, local_rate], axis=1), ((0, 0), (0, LANES - 2)))
    ends = logs.reshape(heads, rows, SPAN)[:, :, -1].T
    seg_ids = info[:, 0]
    unbroken = (seg_ids[:, LANES - 1] == seg_ids[:, LANES + SPAN - 1]).astype(f32)
    keep = jnp.exp(ends) * unbroken[:, None]
    keep_other = sibling(jnp.pad(keep, ((0, 0), (0, LANES - heads))))[:, :heads]
    keep, keep_other = keep[:, :, None, None], keep_other[:, :, None, None]
    keep_plane = keep * keep_other

    all_taps = jnp.concatenate([conv_weight, conv_bias[None]], axis=0)
    taps = jnp.concatenate(
        [lax.dynamic_slice_in_dim(all_taps, row * width, width, 1), all_taps[:, DIN:]], axis=1
    )
    taps = jnp.pad(taps.T, ((0, 0), (0, LANES - TAPS - 1)))

    raw = mm(main_weight[:, :channels], plane_in, CROSS, bf16)
    halo = mm(main_weight[:, :channels], halo_in, CROSS, bf16)
    until(raw, halo_in, gate_parts[1])
    gate_parts.append(up_ring(now(gate_parts[1])))
    halo_in = jnp.pad(now(halo_in), ((0, LANES - 4 * rows), (0, 0)))
    halo = mm(main_weight[:, :channels], halo_in, CROSS, bf16)
    shape = jax.ShapeDtypeStruct
    info_spec = cell_spec(info.shape[1:])
    state_spec = cell_spec((width, NSTATE))
    states = shape((rows, width, NSTATE), bf16)
    by_head = (rows, heads, HDIM, NSTATE)
    row_spec = token_spec(heads)
    wide = token_spec(width)
    tall = token_spec(channels)
    low_wide = shape((width, count), bf16)
    conv, slope, local_state = call(
        conv_kernel, rows, (raw, halo, info, steps, logs, taps),
        [tall, fixed_spec(halo.shape), info_spec, row_spec, row_spec, fixed_spec(taps.shape)],
        [shape((channels, count), bf16), shape((channels, count), bf16), states],
        [tall, tall, state_spec],
        [pltpu.VMEM((width, SPAN), bf16)], name="conv",
    )

    until(local_state, gate_parts[2], cot_x, cot_y)

    def pass_states(mine, hops, beside, near, other):
        is_near = core == near

        def own_heads(a):
            return lax.dynamic_slice_in_dim(a, core * (heads // 2), heads // 2, 1).astype(f32)

        total = own_heads(jnp.where(is_near, other, mine)) + own_heads(
            jnp.where(is_near, keep_other, keep)
        ) * own_heads(jnp.where(is_near, mine, other))
        keep_half = own_heads(keep_plane)
        got = jnp.zeros((), f32)
        for hop, step in zip(hops, beside):
            running = now((total + keep_half * got).astype(bf16))
            until(running)
            passed = over_heads(running, hop)
            until(passed, *step())
            got = got + passed.astype(f32)
        got = now(got.astype(bf16))
        rest = sibling(got)
        whole = by_core(
            jnp.concatenate([got, rest], axis=1), jnp.concatenate([rest, got], axis=1)
        )
        through = (other.astype(f32) + keep_other * whole.astype(f32)).astype(bf16)
        return jnp.where(is_near, whole, through).reshape(states.shape)

    seen = {}

    def within_step():
        seen["within"] = call(
            within_kernel, rows, (conv, info, logs, now(shifted_logs)),
            [tall, info_spec, row_spec, row_spec],
            shape((width, count), f32), wide, name="within",
        )
        for _ in range(planes - 3):
            gate_parts.append(up_ring(now(gate_parts[-1])))
        seen["far"] = across_rows(now(cot_x[:cut]), 2), across_rows(now(cot_y[cut:]), 1)
        return (seen["within"], gate_parts[-1]) + seen["far"]

    def gate_step():
        others = [sibling(now(part)) for part in gate_parts]
        gate_weight = place_parts(
            zeros((width_in, width), others[0]), list(zip(gate_parts, others))
        )
        seen["gate_weight"] = gate_weight
        seen["gate"] = mm(gate_weight, now(plane_in), CROSS)
        for _ in range(planes - 3):
            out_parts.append(up_ring(now(out_parts[-1])))
        return seen["gate"], out_parts[-1]

    def hat_step():
        far = now(*seen["far"])
        seen["cot"], _ = of_plane(far[0], cotangent, cot_x, cot_y, *far)
        out_others = [sibling(now(part)) for part in out_parts]
        seen["out_rank"] = place_parts(
            zeros((width, width_in), far[0]), list(zip(out_parts, out_others))
        )
        seen["hat"] = mm(seen["out_rank"], seen["cot"], NT, bf16)
        return (seen["hat"],)

    local_state = local_state.reshape(by_head)
    other_state = sibling(now(local_state))
    until(other_state)
    state_in = pass_states(
        local_state, [hop_up(p) for p in range(planes - 1)], [within_step, gate_step, hat_step], 0,
        other_state,
    )
    within, gate, grad_hat = seen["within"], seen["gate"], seen["hat"]
    gate_weight, plane_cot, out_rank = seen["gate_weight"], seen["cot"], seen["out_rank"]

    mixed, sums = call(
        mix_kernel, rows, (conv, info, logs, state_in, within, gate, grad_hat, params, rank_gain),
        [tall, info_spec, row_spec, state_spec, wide, wide, wide, fixed_spec(params.shape),
         fixed_spec(rank_gain.shape)],
        [low_wide, shape((8, count), f32)], [wide, token_spec(8)], name="mix",
    )
    sums = sums + sum(across_rows(sums, m) for m in range(1, rows))

    gated_hat, dmixed, dgate, local_dstate = call(
        gate_kernel, rows, (conv, info, logs, mixed, gate, grad_hat, sums, rank_gain),
        [part_spec((2 * NSTATE, SPAN), lambda c: width // (2 * NSTATE), True), info_spec, row_spec,
         wide, wide, wide, token_spec(8), fixed_spec(rank_gain.shape)],
        [low_wide] * 3 + [states], [wide, wide, wide, state_spec],
        [pltpu.VMEM((width, SPAN), bf16)], name="gate",
    )

    def to_owner(partial_sum):
        got = lax.all_to_all(partial_sum.reshape(rows, SPAN, -1), "row", 0, 0, tiled=True)
        return jnp.sum(got.astype(f32), axis=0)

    def rows_product(grads):
        return mm(plane_in, grads, CROSS, bf16)

    def over_planes(product):
        return lax.psum_scatter(product, "head", scatter_dimension=0, tiled=True)

    def dgate_step():
        seen["dgate"] = rows_product(now(dgate))
        out = mm(now(gated_hat), out_rank, TN, bf16)
        seen["out"] = lax.psum_scatter(out, "row", scatter_dimension=0, tiled=True)
        return seen["dgate"], out

    def within_back_step():
        seen["back"] = call(
            within_back_kernel, rows, (conv, info, logs, shifted_logs, now(dmixed), state_in),
            [tall, info_spec, row_spec, row_spec, wide, state_spec],
            [shape((width, count), f32), shape((2 * NSTATE, count), f32),
             shape((3 * heads, count), f32)],
            [wide, token_spec(2 * NSTATE), token_spec(3 * heads)],
            [pltpu.VMEM((width, SPAN), bf16), pltpu.VMEM((LANES, LANES), f32),
             pltpu.VMEM((SPAN, LANES), f32)],
            name="within_back",
        )
        return seen["back"][:1]

    def out_step():
        seen["dout"] = mm(now(gated_hat), plane_cot, NN, bf16)
        return seen["dout"], seen["out"]

    local_dstate = local_dstate.reshape(by_head)
    other_dstate = sibling(local_dstate)
    until(other_dstate)
    dstate_out = pass_states(
        local_dstate, [hop_down(p) for p in reversed(range(planes - 1))],
        [dgate_step, within_back_step, out_step], 1, other_dstate,
    )
    dx, dmatrix, row_sums = seen["back"]
    seen["dgate_sum"] = over_planes(now(seen["dgate"]))
    output = (activations + seen["out"].astype(f32)).astype(bf16)

    grad_conv, dsteps, grad_starts = call(
        state_back_kernel, rows,
        (conv, slope, info, logs, steps, step_slope, dmixed, dx, dmatrix, row_sums, dstate_out,
         state_in, params),
        [tall, tall, info_spec, row_spec, row_spec, row_spec, wide, wide, token_spec(2 * NSTATE),
         token_spec(3 * heads), state_spec, state_spec, fixed_spec(params.shape)],
        [shape((channels, count), bf16), shape((2 * heads, count), f32),
         shape((channels, LANES), bf16)],
        [tall, token_spec(2 * heads), fixed_spec((channels, LANES))],
        [pltpu.VMEM((width, SPAN), bf16)], name="state_back",
    )
    until(grad_starts)

    dout = now(seen["dout"]).reshape(groups, planes, 2, out_rows, width_in)
    dout_mine = by_core(dout[:, :, 0], dout[:, :, 1])
    dout_other = sibling(by_core(dout[:, :, 1], dout[:, :, 0]))
    next_starts = over_heads(now(grad_starts), last_span)
    seen["gate_part"] = mm(now(dgate), gate_weight, CROSS, bf16)
    until(next_starts, seen["gate_part"])

    def out_piece(i):
        at = (plane - i) % planes
        return sum(
            lax.dynamic_index_in_dim(a, at, 1, keepdims=False).astype(f32)
            for a in (dout_mine, dout_other)
        )

    def head_exchange(dtaps):
        taps_sum = jnp.sum(dtaps, axis=2).reshape(-1)
        head_sums = jnp.sum(jnp.concatenate([dsteps, row_sums[2 * heads :]], axis=0), axis=1)
        packed = jnp.concatenate([taps_sum, head_sums])
        padded = -(-packed.shape[0] // (8 * LANES)) * 8 * LANES
        packed = jnp.pad(packed, (0, padded - packed.shape[0])).reshape(padded // LANES, LANES)
        packed = jnp.broadcast_to(packed[None], (head_axis,) + packed.shape)
        return lax.all_to_all(packed, "head", 0, 0, tiled=True)

    def conv_back_step():
        seen["draw"], seen["dtaps"] = call(
            conv_back_kernel, rows, (raw, halo, now(grad_conv), next_starts, info, taps),
            [tall, fixed_spec(halo.shape), tall, fixed_spec(grad_starts.shape), info_spec,
             fixed_spec(taps.shape)],
            [shape((channels, count), bf16), shape((TAPS + 1, channels, LANES), f32)],
            [tall, fixed_spec((TAPS + 1, channels, LANES))], name="conv_back",
        )
        return (seen["draw"],)

    def grad_part(i):
        lanes = slice(i * half, (i + 1) * half)
        part = mm(now(seen["dmain"]), main_weight[lanes], CROSS)
        return (part + seen["gate_part"][:, lanes].astype(f32)).astype(bf16)

    grad_parts, gate_rows = [], []
    def next_sum(i, *since):
        passed = over_heads(tie(running.astype(bf16), *since)[0], ring_down)
        return passed, passed.astype(f32) + out_piece(i)

    running = out_piece(planes - 1)
    passed, running = next_sum(planes - 2, next_starts)
    until(*conv_back_step())
    seen["dmain"] = jnp.concatenate([now(seen["draw"]), dsteps[:heads].astype(bf16)], axis=0)
    product = rows_product(seen["dmain"])
    dmain_sum = over_planes(tie(product, seen["dgate_sum"])[0])
    until(product)
    first_part = grad_part(0)
    grad_parts.append(to_owner(first_part))
    sums = tie(seen["dgate_sum"], product)[0].reshape(rows, span_rows, -1)
    for m in range(rows):
        part = lax.dynamic_index_in_dim(sums, row ^ m, 0, keepdims=False)
        gate_rows.append(across_rows(part, m) if m else part)
    second_part = grad_part(1)
    for i in reversed(range(planes - 2)):
        passed, running = next_sum(i, second_part if i else grad_parts[0])
    params = jnp.sum(head_exchange(tie(seen["dtaps"], grad_parts[0], second_part)[0]), axis=0)
    grad_parts.append(to_owner(tie(second_part, params)[0]))
    seen["others"] = [across_rows(params, m) for m in range(1, rows)]
    dmain_rows = tie(dmain_sum, grad_parts[1], *gate_rows, *seen["others"])[0]
    dmain_rows = lax.all_to_all(
        dmain_rows.reshape(rows, span_rows, -1), "row", 0, 0, tiled=True
    )
    if groups > 1:
        running = lax.psum_scatter(
            running, "head", scatter_dimension=0, axis_index_groups=same_place, tiled=True
        )
    out_weight_grad = running.reshape(out_rows, width_in)
    gate_gain_grad = jnp.sum(out_weight_grad * out_weight.astype(f32), axis=1) / gate_gain.astype(f32)

    every = jnp.zeros((rows, params.size), f32)
    for m, part in enumerate([params] + seen["others"]):
        every = lax.dynamic_update_slice(every, part.reshape(1, -1), (row ^ m, 0))
    total = every

    normed_arranged, cot_arranged = arranged(normed), arranged(cotangent)
    grad_normed = jnp.concatenate(grad_parts, axis=1) * gain_arranged
    grad_tokens = inverse * (
        grad_normed
        - normed_arranged * jnp.mean(grad_normed * normed_arranged, axis=-1, keepdims=True)
    )
    input_grad = restored((cot_arranged.astype(f32) + grad_tokens).astype(bf16))

    tail = dmain_rows[..., channels:].transpose(1, 0, 2).reshape(span_rows, HEADS)
    place = jnp.reshape(row, (1,)).astype(jnp.int32)
    in_weight_grad, norm_sums = finish(place, gate_rows, dmain_rows, tail, in_weight)
    norm_gain_grad = jnp.sum(norm_sums, axis=1) / norm_gain.astype(f32)

    taps_size, size = (TAPS + 1) * channels, (TAPS + 1) * channels + 3 * heads
    total_taps = total[:, :taps_size].reshape(rows, TAPS + 1, channels)
    all_taps_grad = jnp.concatenate(
        [
            total_taps[..., :width].transpose(1, 0, 2).reshape(TAPS + 1, DIN),
            jnp.sum(total_taps[..., width:], axis=0),
        ],
        axis=1,
    )
    total_heads = total[:, taps_size:size].reshape(rows, 3, heads)
    total_heads = total_heads.transpose(1, 0, 2).reshape(3, HEADS)
    return (
        output,
        input_grad,
        in_weight_grad,
        norm_gain_grad,
        out_weight_grad,
        gate_gain_grad,
        all_taps_grad[:TAPS],
        all_taps_grad[TAPS],
        total_heads[0],
        total_heads[1],
        total_heads[2],
    )


def solution(mesh):
    both = ("row", "head")
    return jax.shard_map(
        shards,
        mesh=mesh,
        in_specs=(
            P(both, None), P(both, None), P(both), P(both, None), P(both),
            P(), P(), P(), P(), P(),
            P("row", None), P("row"), P(both, None),
        ),
        out_specs=(
            P(both, None), P(both, None), P(both, None), P(both), P(both, None), P(both),
            P(), P(), P(), P(), P(),
        ),
        check_vma=False,
    )
```
